32 devices in a mesh: dp: 4 (over z), blk: 8 (over y, x, core).
Axes of the slice: x: 2, y: 2, z: 4, core: 2. Of those that a mesh axis runs over, the one named last changes fastest.
Arguments:
- noise: bfloat16 [640, 8192], P('blk', 'dp'), may hold values from -1 to 1
- buffer: bfloat16 [640, 32768], P('blk', 'dp'), may hold values from -6 to 6
- reinit: int32 [128], P('dp'), may hold values 0 or 1
- slots: int32 [128], P('dp'), may hold values from 0 to 127
- kernel_one: bfloat16 [9, 640, 640], P(None, 'blk'), may hold values from -0.078125 to 0.078125
- bias_one: bfloat16 [640], P('blk'), may hold values from -3 to 3
- kernel_two: bfloat16 [9, 640, 640], P(None, 'blk'), may hold values from -0.078125 to 0.078125
- bias_two: bfloat16 [640], P('blk'), may hold values from -3 to 3
- cotangent: bfloat16 [640, 8192], P('blk', 'dp'), may hold values from -6 to 6
Outputs:
- output: bfloat16 [640, 8192], P('blk', 'dp')
- grad_field: float32 [640, 8192], P('blk', 'dp')
- grad_kernel_one: float32 [9, 640, 640], P(None, 'blk')
- grad_bias_one: float32 [640], P('blk')
- grad_kernel_two: float32 [9, 640, 640], P(None, 'blk')
- grad_bias_two: float32 [640], P('blk')
The draws below stay inside these ranges and needn't reach their ends.
All inputs are finite; a program needn't handle non-finite values. No bound on the sum of `reinit` on one device may be relied on, other than what follows from the above.
Results may differ from the reference program's by a relative error of at most 0.0055.
Values may be sent and summed in bfloat16 or wider, within the bound.
No kernel may reach another device: no remote copies, remote signals or barrier semaphores. Data moves between devices by JAX's collectives and lax.ppermute only.
A program may use at most 192 MiB of HBM per device.

```python
import jax
import jax.numpy as jnp
from jax import lax

C = 640
IMG_DEV = 32
BUF_DEV = 128
IMAGES = 128
PIXELS = 8192
SLOTS = 512


def touch_ends(values, stream_key, smallest, top_value):
    longest = values.shape.index(max(values.shape))
    spots = []
    for shift in (0, 1):
        where = [jax.random.randint(jax.random.fold_in(stream_key, axis), (), 0, length) for axis, length in enumerate(values.shape)]
        where[longest] = (where[longest] + shift) % values.shape[longest]
        spots.append(tuple(where))
    return values.at[spots[0]].set(smallest).at[spots[1]].set(top_value)


def steps_of(stream_key, dims, shards, low, largest):
    factor_of, own = 1.0, jax.random.fold_in(stream_key, 6)
    for axis_at, parts in shards:
        steps = jnp.exp(jax.random.uniform(jax.random.fold_in(own, axis_at), (parts,), jnp.float32, low / len(shards), largest / len(shards)))
        factor_of = factor_of * jnp.repeat(steps, dims[axis_at] // parts).reshape([-1 if axis == axis_at else 1 for axis in range(len(dims))])
    return factor_of


def bell_draw(stream_key, shape, deviation, bound, shards=(), kind=jnp.bfloat16):
    level = steps_of(stream_key, shape, shards, -0.22, 0.18) if shards else 1.0
    result = jax.random.normal(stream_key, shape, jnp.float32) * deviation * level
    return jnp.minimum(jnp.maximum(result, -bound), bound).astype(kind)


def setup_inputs(seed: int = 0) -> dict:
    streams_of = jax.random.split(jax.random.key(seed), 10)
    return {
        "noise": jnp.clip(jax.random.uniform(streams_of[0], (C, PIXELS), jnp.float32, -1.0, 1.0) * steps_of(streams_of[0], (C, PIXELS), ((0, 8), (1, 4)), -0.4, 0.0), -1.0, 1.0).astype(jnp.bfloat16),
        "buffer": bell_draw(streams_of[1], (C, SLOTS * 64), 1.0, 6.0, ((0, 8), (1, 4))),
        "reinit": touch_ends((jax.random.randint(streams_of[2], (IMAGES,), 0, 8) < 1).astype(jnp.int32), jax.random.fold_in(streams_of[2], 1), 0, 1),
        "slots": touch_ends(jax.random.randint(streams_of[3], (IMAGES,), 0, BUF_DEV), jax.random.fold_in(streams_of[3], 1), 0, BUF_DEV - 1).astype(jnp.int32),
        "kernel_one": bell_draw(streams_of[4], (9, C, C), (9 * C) ** -0.5, 0.078125, ((1, 8),)),
        "bias_one": bell_draw(streams_of[5], (C,), 0.5, 3.0, ((0, 8),)),
        "kernel_two": bell_draw(streams_of[6], (9, C, C), (9 * C) ** -0.5, 0.078125, ((1, 8),)),
        "bias_two": bell_draw(streams_of[7], (C,), 0.5, 3.0, ((0, 8),)),
        "cotangent": bell_draw(streams_of[8], (C, PIXELS), 1.0, 6.0, ((0, 8), (1, 4))),
    }


@jax.custom_vjp
def low(v):
    return lax.optimization_barrier(v.astype(jnp.bfloat16)).astype(jnp.float32)

@jax.custom_vjp
def low_back(v):
    return v

def low_keep(v):
    return (low(v), None)

def low_pass(kept, grad):
    return (grad,)

def back_keep(v):
    return (v, None)

def back_low(kept, grad):
    return (low(grad),)
low.defvjp(low_keep, low_pass)
low_back.defvjp(back_keep, back_low)
offsets = [(row, col) for row in (-1, 0, 1) for col in (-1, 0, 1)]

def shift_tap(field, row, col):
    depth = field.shape[0]
    grid = field.reshape(depth, -1, 8, 8)
    grid = jnp.pad(grid, ((0, 0), (0, 0), (1, 1), (1, 1)))
    grid = grid[:, :, 1 + row:9 + row, 1 + col:9 + col]
    return grid.reshape(depth, -1)

def convolve(field, kernel):
    total = jnp.zeros((kernel.shape[1], field.shape[1]), jnp.float32)
    for number, (row, col) in enumerate(offsets):
        total = total + jnp.dot(kernel[number], shift_tap(field, row, col), precision=lax.Precision.HIGHEST)
    return total

def assemble(noise, buffer, reinit, slots):
    images = reinit.shape[0]
    group = (jnp.arange(images, dtype=jnp.int32) // IMG_DEV).astype(jnp.int32)
    where_slot = (group * BUF_DEV + slots).astype(jnp.int32)
    stored = buffer.astype(jnp.float32).reshape(C, -1, 64)[:, where_slot, :]
    fresh = noise.astype(jnp.float32).reshape(C, images, 64)
    chosen = jnp.where(reinit[None, :, None] == 1, fresh, stored)
    return chosen.reshape(C, images * 64)

def forward(field, kernel_one, bias_one, kernel_two, bias_two):
    act_zero = low(jax.nn.silu(field))
    pre_one = low_back(convolve(act_zero, kernel_one) + bias_one[:, None])
    act_one = low(jax.nn.silu(pre_one))
    return field + convolve(act_one, kernel_two) + bias_two[:, None]

def reference(noise, buffer, reinit, slots, kernel_one, bias_one, kernel_two, bias_two, cotangent):
    field = assemble(noise, buffer, reinit, slots)
    output, pull = jax.vjp(forward, field, kernel_one.astype(jnp.float32), bias_one.astype(jnp.float32), kernel_two.astype(jnp.float32), bias_two.astype(jnp.float32))
    grads = pull(cotangent.astype(jnp.float32))
    return (output.astype(jnp.bfloat16), grads[0], grads[1], grads[2], grads[3], grads[4])
```

```python
import functools

import jax
import jax.numpy as jnp
from jax import lax
from jax.experimental import pallas as pl
from jax.experimental.pallas import tpu as pltpu
from jax.sharding import PartitionSpec as P

bf16 = jnp.bfloat16
f32 = jnp.float32
offsets = [(row, col) for row in (-1, 0, 1) for col in (-1, 0, 1)]
VMEM_LIMIT = 40 << 20
EXTRA = 16
TILE = 256


def silu_slope(value):
    sigma = jax.nn.sigmoid(value)
    return sigma * (1.0 + value * (1.0 - sigma))


def inside(width, row, col):
    pixel = lax.broadcasted_iota(jnp.int32, (1, width), 1)
    r = ((pixel >> 3) & 7) + row
    s = (pixel & 7) + col
    return (r >= 0) & (r < 8) & (s >= 0) & (s < 8)


def shifted(values, row, col):
    step = 8 * row + col
    if step == 0:
        return values
    width = values.shape[1]
    moved = pltpu.roll(values, (-step) % width, 1)
    return jnp.where(inside(width, row, col), moved, jnp.zeros_like(moved))


def field_kernel(core, reinit, slots, noise, buffer, cotangent, bias, field, send, keep):
    half = field.shape[1] // 2
    lane = lax.broadcasted_iota(jnp.int32, (1, 128), 1)
    me = core[0]
    other = 1 - me

    def place(image, block):
        slot = slots[image]
        start = pl.multiple_of((slot >> 1) * 128, 128)
        stored = buffer[:, pl.ds(start, 128)].astype(f32)
        turned = pltpu.roll(stored, 64, 1)
        stored = jnp.where((slot & 1) == (image & 1), stored, turned)
        return jnp.where(reinit[image] == 1, block, stored)

    for pair in range(field.shape[1] // 128):
        here = pl.ds(pair * 128, 128)
        block = noise[:, here].astype(f32)
        left = place(2 * pair, block)
        right = place(2 * pair + 1, block)
        value = jnp.where(lane < 64, left, right)
        field[:, here] = value.astype(bf16)
        act = (value * jax.nn.sigmoid(value)).astype(bf16)
        owner = (pair * 128) // half
        inner = pl.ds(pair * 128 - owner * half, 128)

        @pl.when(me == owner)
        def _():
            keep[:, inner] = act

        @pl.when(me != owner)
        def _():
            send[:, inner] = act

    tail = pl.ds(half, half)
    keep[:, tail] = cotangent[:, pl.ds(pl.multiple_of(me * half, 128), half)]
    send[:, tail] = cotangent[:, pl.ds(pl.multiple_of(other * half, 128), half)]
    column = jnp.broadcast_to(bias[...].astype(f32), (field.shape[0], 128)).astype(bf16)
    keep[:, pl.ds(2 * half, 128)] = column
    send[:, pl.ds(2 * half, 128)] = column


def write_shifts(stack, values):
    depth = values.shape[0]
    for tap, (row, col) in enumerate(offsets):
        stack[pl.ds(tap * depth, depth), :] = shifted(values, -row, -col)


def write_back(order, block, kernels, stacks, send, keep):
    half, pixels = keep.shape[0], keep.shape[2]

    def step(at, _):
        lanes = pl.ds(pl.multiple_of(at * TILE, TILE), TILE)
        total = None
        for kernel, stack in zip(kernels, stacks):
            part = lax.dot_general(
                kernel[...], stack[:, lanes], (((0,), (0,)), ((), ())), preferred_element_type=f32
            )
            total = part if total is None else total + part
        block[...] = total
        depth = keep.shape[1]
        for slot in range(2 * half):
            rows = block[pl.ds(pl.multiple_of(order[slot] * depth, 8), depth), :]
            if slot < half:
                keep[slot, :, lanes] = rows
            else:
                send[slot - half, :, lanes] = rows.astype(bf16)
        return 0

    lax.fori_loop(0, pixels // TILE, step, 0)


def back_two_kernel(order, own, other, kernel_own, kernel_other, stack_own, stack_other, send, keep, block):
    write_shifts(stack_own, own[...])
    write_shifts(stack_other, other[...])
    write_back(order, block, (kernel_own, kernel_other), (stack_own, stack_other), send, keep)


def back_one_kernel(order, kernel_own, kernel_other, stack_own, stack_other, send, keep, block):
    write_back(order, block, (kernel_own, kernel_other), (stack_own, stack_other), send, keep)


def fetch(order, pieces, whole, sem):
    copies, slot = [], 0
    for piece in pieces:
        count, depth = piece.shape[0], piece.shape[1]
        for at in range(count):
            start = pl.multiple_of(order[slot] * depth, 16)
            copies.append(
                pltpu.make_async_copy(piece.at[at], whole.at[pl.ds(start, depth), :], sem.at[slot])
            )
            slot += 1
    for copy in copies:
        copy.start()
    for copy in copies:
        copy.wait()


def conv_tile(kernel, tile):
    depth = kernel.shape[0] // 9
    spread = jnp.dot(kernel[...], tile, preferred_element_type=f32)
    total = spread[4 * depth : 5 * depth]
    for tap, (row, col) in enumerate(offsets):
        if tap != 4:
            total = total + shifted(spread[tap * depth : (tap + 1) * depth], row, col)
    return total


def conv_one_kernel(
    core, order, own, near, far, kernel_own, kernel_other, bias_own, bias_other, whole, pre_own, pre_other, act, sem
):
    fetch(order, (own, near, far), whole, sem)
    depth = pre_own.shape[0]

    def step(at, _):
        lanes = pl.ds(pl.multiple_of(at * TILE, TILE), TILE)
        tile = whole[:, lanes]
        for kernel, bias, pre, place in (
            (kernel_own, bias_own, pre_own, core[0]),
            (kernel_other, bias_other, pre_other, 1 - core[0]),
        ):
            value = conv_tile(kernel, tile) + bias[:, :1].astype(f32)
            pre[:, lanes] = value
            rows = pl.ds(pl.multiple_of(place * depth, 16), depth)
            act[rows, lanes] = (value * jax.nn.sigmoid(value)).astype(bf16)
        return 0

    lax.fori_loop(0, whole.shape[1] // TILE, step, 0)


def conv_two_kernel(whole, kernel_own, kernel_other, out_own, out_other):
    def step(at, _):
        lanes = pl.ds(pl.multiple_of(at * TILE, TILE), TILE)
        tile = whole[:, lanes]
        out_own[:, lanes] = conv_tile(kernel_own, tile)
        out_other[:, lanes] = conv_tile(kernel_other, tile)
        return 0

    lax.fori_loop(0, whole.shape[1] // TILE, step, 0)


def write_kernel_grad(stack, whole, grad):
    rows = stack.shape[0]
    depth = rows // 9
    transposed = (((1,), (1,)), ((), ()))
    grad[:rows, :] = lax.dot_general(
        stack[...], whole[...], transposed, preferred_element_type=f32
    ).astype(grad.dtype)
    ones = jnp.ones((EXTRA, stack.shape[1]), bf16)
    sums = lax.dot_general(
        ones, stack[4 * depth : 5 * depth, :], transposed, preferred_element_type=f32
    )
    grad[rows:, :] = jnp.zeros((EXTRA, grad.shape[1]), grad.dtype)
    grad[rows:, :depth] = sums.astype(grad.dtype)


def grad_one_kernel(
    core, kept, near, far, pre_own, pre_other, whole, stack_own, stack_other, grad_own, grad_other
):
    depth = pre_own.shape[0]
    for pre, place, stack in (
        (pre_own, core[0], stack_own),
        (pre_other, 1 - core[0], stack_other),
    ):
        rows = pl.ds(pl.multiple_of(place * depth, 16), depth)
        upstream = kept[0, rows, :] + near[0, rows, :].astype(f32) + far[0, rows, :].astype(f32)
        write_shifts(stack, (upstream * silu_slope(pre[...])).astype(bf16))
    write_kernel_grad(stack_other, whole, grad_other)
    write_kernel_grad(stack_own, whole, grad_own)


def grad_two_kernel(order, own, near, far, stack_own, stack_other, whole, grad_own, grad_other, sem):
    fetch(order, (own, near, far), whole, sem)
    write_kernel_grad(stack_other, whole, grad_other)
    write_kernel_grad(stack_own, whole, grad_own)


def finish_kernel(places, quarter, near, far, grad, bias, total, sem):
    size = quarter.shape[0]
    for piece, at, place in (
        (quarter, None, places[0]),
        (near, None, places[1]),
        (far, 0, places[2]),
        (far, 1, places[3]),
    ):
        rows = pl.ds(pl.multiple_of(place * size, 8), size)
        total[rows, :] = (piece[...] if at is None else piece[at]).astype(f32)
    copy = pltpu.make_async_copy(total.at[pl.ds(0, grad.shape[0]), :], grad, sem)
    copy.start()
    bias[...] = total[grad.shape[0] :, :]
    copy.wait()


SMEM = pl.BlockSpec(memory_space=pltpu.SMEM)
VMEM = pl.BlockSpec(memory_space=pltpu.VMEM)
ANY = pl.BlockSpec(memory_space=pl.ANY)


def run(body, name, ins, outs, scratch=(), flops=0, out_specs=None):
    specs, args = zip(*ins)
    moved = sum(a.size * a.dtype.itemsize for a in args) + sum(
        o.size * o.dtype.itemsize for o in outs
    )
    return pl.pallas_call(
        body,
        name=name,
        out_shape=outs,
        in_specs=list(specs),
        out_specs=out_specs or [VMEM] * len(outs),
        scratch_shapes=list(scratch),
        cost_estimate=pl.CostEstimate(flops=flops, bytes_accessed=moved, transcendentals=0),
        compiler_params=pltpu.CompilerParams(vmem_limit_bytes=VMEM_LIMIT),
    )(*args)


def split_local(
    groups, width, noise, buffer, reinit, slots, kernel_one, bias_one, kernel_two, bias_two, cotangent
):
    depth, pixels = noise.shape
    channels = kernel_one.shape[2]
    half = pixels // 2
    chips = width // 2
    block = 2 * depth
    rows = 9 * depth
    work = 2 * 2 * rows * channels * half
    index = lax.axis_index("blk")
    core = index % 2
    chip = index // 2
    group = lax.axis_index("dp")
    shape = jax.ShapeDtypeStruct

    first = [2, 4]

    def chip_swap(values, step):
        pairs = [(i, i ^ first[(step + i) % 2]) for i in range(width)]
        return lax.ppermute(values, "blk", pairs)

    def core_swap(values):
        return lax.ppermute(values, "blk", [(i, i ^ 1) for i in range(width)])

    def group_swap(values, bit):
        return lax.ppermute(values, "dp", [(i, i ^ bit) for i in range(groups)])

    masks = jnp.where(core == 0, jnp.array([0, 1, 2, 3]), jnp.array([0, 2, 1, 3]))
    order = jnp.bitwise_xor(chip, masks).astype(jnp.int32)
    core_at = core.reshape(1).astype(jnp.int32)

    def gather(own):
        near = chip_swap(own, 0)
        far = chip_swap(jnp.concatenate([own, near], 0), 1)
        return own, near, far

    def scatter(send, keep):
        near = chip_swap(send, 1)
        far = chip_swap((keep[1:] + near[1:].astype(f32)).astype(bf16), 0)
        return keep, near, far

    own_one = kernel_one.reshape(rows, channels)
    own_two = kernel_two.reshape(rows, channels)
    other_two = core_swap(own_two)
    other_one = core_swap(own_one)

    field, send, keep = run(
        field_kernel,
        "field",
        [
            (SMEM, core_at),
            (SMEM, reinit),
            (SMEM, slots),
            (VMEM, noise),
            (VMEM, buffer),
            (VMEM, cotangent),
            (VMEM, bias_one[:, None]),
        ],
        [
            shape((depth, pixels), bf16),
            shape((depth, pixels + 128), bf16),
            shape((depth, pixels + 128), bf16),
        ],
    )
    came = core_swap(send)

    def paired(ours, theirs):
        return jnp.where(
            core == 0, jnp.concatenate([ours, theirs], 0), jnp.concatenate([theirs, ours], 0)
        )

    act_zero = paired(keep[:, :half], came[:, :half])[None]
    zero = gather(act_zero)

    stack = shape((rows, half), bf16)
    sends = shape((chips // 2, block, half), bf16)
    keeps = shape((chips // 2, block, half), f32)
    wide = pltpu.VMEM((channels, TILE), f32)
    cot_own, cot_other, send_two, keep_two = run(
        back_two_kernel,
        "back_two",
        [
            (SMEM, order),
            (VMEM, keep[:, half : 2 * half]),
            (VMEM, came[:, half : 2 * half]),
            (VMEM, own_two),
            (VMEM, other_two),
        ],
        [stack, stack, sends, keeps],
        [wide],
        work,
    )
    grad_act = scatter(send_two, keep_two)

    whole = shape((channels, half), bf16)
    plane = shape((depth, half), f32)
    whole_zero, pre_own, pre_other, act_one = run(
        conv_one_kernel,
        "conv_one",
        [
            (SMEM, core_at),
            (SMEM, order),
            (ANY, zero[0]),
            (ANY, zero[1]),
            (ANY, zero[2]),
            (VMEM, own_one),
            (VMEM, other_one),
            (VMEM, keep[:, 2 * half :]),
            (VMEM, came[:, 2 * half :]),
        ],
        [whole, plane, plane, shape((block, half), bf16)],
        [pltpu.SemaphoreType.DMA((chips,))],
        work,
    )
    one = gather(act_one[None])

    grad = [shape((rows + EXTRA, channels), f32), shape((rows + EXTRA, channels), bf16)]
    pre_stack_own, pre_stack_other, grad_one, grad_one_other = run(
        grad_one_kernel,
        "grad_one",
        [
            (SMEM, core_at),
            (VMEM, grad_act[0][:1]),
            (VMEM, grad_act[1][:1]),
            (VMEM, grad_act[2]),
            (VMEM, pre_own),
            (VMEM, pre_other),
            (VMEM, whole_zero),
        ],
        [stack, stack] + grad,
        (),
        work,
    )
    came_one = core_swap(grad_one_other)

    send_one, keep_one = run(
        back_one_kernel,
        "back_one",
        [
            (SMEM, order),
            (VMEM, own_one),
            (VMEM, other_one),
            (VMEM, pre_stack_own),
            (VMEM, pre_stack_other),
        ],
        [sends, keeps],
        [wide],
        work,
    )
    grad_zero = scatter(send_one, keep_one)

    whole_one, grad_two, grad_two_other = run(
        grad_two_kernel,
        "grad_two",
        [
            (SMEM, order),
            (ANY, one[0]),
            (ANY, one[1]),
            (ANY, one[2]),
            (VMEM, cot_own),
            (VMEM, cot_other),
        ],
        [whole] + grad,
        [pltpu.SemaphoreType.DMA((chips,))],
        work,
    )
    came_two = core_swap(grad_two_other)

    out_own, out_other = run(
        conv_two_kernel,
        "conv_two",
        [(VMEM, whole_one), (VMEM, own_two), (VMEM, other_two)],
        [plane, plane],
        (),
        work,
    )

    def unsplit(ours, theirs):
        return jnp.where(
            core == 0, jnp.concatenate([ours, theirs], 1), jnp.concatenate([theirs, ours], 1)
        )

    held = field.astype(f32)
    output = held + unsplit(out_own, core_swap(out_other)) + bias_two.astype(f32)[:, None]
    output = output.astype(bf16)

    total = grad_zero[0][0] + grad_zero[1][0].astype(f32) + grad_zero[2][0].astype(f32)
    ours = lax.dynamic_slice_in_dim(total, core * depth, depth, 0)
    theirs = lax.dynamic_slice_in_dim(total, (1 - core) * depth, depth, 0)
    grad_act_zero = unsplit(ours, core_swap(theirs))
    grad_field = cotangent.astype(f32) + grad_act_zero * silu_slope(held)

    low, high = group % 2, group // 2
    size = (rows + EXTRA) // 4
    places = jnp.stack(
        [
            low * 2 + high,
            low * 2 + 1 - high,
            (1 - low) * 2,
            (1 - low) * 2 + 1,
        ]
    ).astype(jnp.int32)

    def reduce(ours, theirs):
        ours = ours.reshape(2, 2, size, channels)
        theirs = theirs.reshape(2, 2, size, channels)

        def part(at):
            return lax.dynamic_index_in_dim(
                ours, at, 0, keepdims=False
            ) + lax.dynamic_index_in_dim(theirs, at, 0, keepdims=False).astype(f32)

        near = group_swap(part(1 - low).astype(bf16), 1)
        mine = part(low)

        def piece(at):
            return lax.dynamic_index_in_dim(
                mine, at, 0, keepdims=False
            ) + lax.dynamic_index_in_dim(near, at, 0, keepdims=False).astype(f32)

        far = group_swap(piece(1 - high).astype(bf16), 2)
        quarter = (piece(high) + far.astype(f32)).astype(bf16)
        beside = group_swap(quarter, 2)
        joined = jnp.where(high == 0, jnp.stack([quarter, beside]), jnp.stack([beside, quarter]))
        rest = group_swap(joined, 1)
        kernel_grad, bias_grad = run(
            finish_kernel,
            "finish",
            [(SMEM, places), (VMEM, quarter), (VMEM, beside), (VMEM, rest)],
            [shape((rows, channels), f32), shape((EXTRA, channels), f32)],
            [pltpu.VMEM((rows + EXTRA, channels), f32), pltpu.SemaphoreType.DMA],
            0,
            [ANY, VMEM],
        )
        return kernel_grad.reshape(9, depth, channels), bias_grad[0, :depth]

    kernel_grad_one, bias_grad_one = reduce(grad_one, came_one)
    kernel_grad_two, bias_grad_two = reduce(grad_two, came_two)
    return output, grad_field, kernel_grad_one, bias_grad_one, kernel_grad_two, bias_grad_two


def shift_tap(field, row, col):
    depth = field.shape[0]
    grid = field.reshape(depth, -1, 8, 8)
    grid = jnp.pad(grid, ((0, 0), (0, 0), (1, 1), (1, 1)))
    grid = grid[:, :, 1 + row : 9 + row, 1 + col : 9 + col]
    return grid.reshape(depth, -1)


def add_conv(total, piece, kernel):
    for number, (row, col) in enumerate(offsets):
        total = total + jnp.dot(
            kernel[number], shift_tap(piece, row, col), preferred_element_type=f32
        )
    return total


def add_grad(piece, upstream):
    parts = [
        lax.dot_general(
            upstream,
            shift_tap(piece, row, col),
            (((1,), (1,)), ((), ())),
            preferred_element_type=f32,
        )
        for row, col in offsets
    ]
    return jnp.stack(parts, 0)


def back_shifts(upstream):
    return jnp.stack([shift_tap(upstream, -row, -col) for row, col in offsets], 0)


def spread_rows(kernel, moved):
    return lax.dot_general(kernel, moved, (((0, 1), (0, 1)), ((), ())), preferred_element_type=f32)


def plain_local(
    noise, buffer, reinit, slots, kernel_one, bias_one, kernel_two, bias_two, cotangent
):
    depth = noise.shape[0]
    images = reinit.shape[0]
    pixels = images * 64
    stored = buffer.reshape(depth, -1, 64)[:, slots, :]
    fresh = noise.reshape(depth, images, 64)
    field = (
        jnp.where(reinit[None, :, None] == 1, fresh, stored).reshape(depth, pixels).astype(f32)
    )
    act_zero = jax.nn.silu(field).astype(bf16)
    empty = jnp.zeros((depth, pixels), f32)
    whole_zero = lax.all_gather(act_zero, "blk", axis=0, tiled=True)
    pre_one = add_conv(empty, whole_zero, kernel_one)
    pre_one = pre_one + bias_one.astype(f32)[:, None]
    act_one = jax.nn.silu(pre_one).astype(bf16)
    whole_one = lax.all_gather(act_one, "blk", axis=0, tiled=True)
    pre_two = add_conv(empty, whole_one, kernel_two)
    output = (field + pre_two + bias_two.astype(f32)[:, None]).astype(bf16)
    bias_grad_two = jnp.sum(cotangent.astype(f32), axis=1)
    kernel_grad_two = add_grad(whole_one, cotangent)
    grad_act_one = lax.psum_scatter(
        spread_rows(kernel_two, back_shifts(cotangent)), "blk", scatter_dimension=0, tiled=True
    )
    grad_pre_one = (grad_act_one * silu_slope(pre_one)).astype(bf16)
    bias_grad_one = jnp.sum(grad_pre_one.astype(f32), axis=1)
    kernel_grad_one = add_grad(whole_zero, grad_pre_one)
    grad_act_zero = lax.psum_scatter(
        spread_rows(kernel_one, back_shifts(grad_pre_one)).astype(bf16),
        "blk",
        scatter_dimension=0,
        tiled=True,
    ).astype(f32)
    grad_field = cotangent.astype(f32) + grad_act_zero * silu_slope(field)
    summed = lax.psum((kernel_grad_one, bias_grad_one, kernel_grad_two, bias_grad_two), "dp")
    return (output, grad_field, summed[0], summed[1], summed[2], summed[3])


def solution(mesh):
    groups, width = mesh.shape["dp"], mesh.shape["blk"]

    def local(noise, *rest):
        if groups == 4 and width == 8 and noise.shape[0] % 16 == 0 and noise.shape[1] % 512 == 0:
            return split_local(groups, width, noise, *rest)
        return plain_local(noise, *rest)

    return jax.shard_map(
        local,
        mesh=mesh,
        in_specs=(
            P("blk", "dp"),
            P("blk", "dp"),
            P("dp"),
            P("dp"),
            P(None, "blk", None),
            P("blk"),
            P(None, "blk", None),
            P("blk"),
            P("blk", "dp"),
        ),
        out_specs=(
            P("blk", "dp"),
            P("blk", "dp"),
            P(None, "blk", None),
            P("blk"),
            P(None, "blk", None),
            P("blk"),
        ),
        check_vma=False,
    )
```

```python
import functools

import jax
import jax.numpy as jnp
from jax import lax
from jax.experimental import pallas as pl
from jax.experimental.pallas import tpu as pltpu
from jax.sharding import PartitionSpec as P

bf16 = jnp.bfloat16
f32 = jnp.float32
offsets = [(row, col) for row in (-1, 0, 1) for col in (-1, 0, 1)]
VMEM_LIMIT = 20 << 20
EARLY = (10**10, 0)
LATE = (2 * 10**10, 3 * 10**9)
EXTRA = 16
SPLIT = 5
TILE = 256
CONV_TILE = 512


def silu_slope(value):
    sigma = jax.nn.sigmoid(value)
    return sigma * (1.0 + value * (1.0 - sigma))


def inside(width, row, col):
    pixel = lax.broadcasted_iota(jnp.int32, (1, width), 1)
    r = ((pixel >> 3) & 7) + row
    s = (pixel & 7) + col
    return (r >= 0) & (r < 8) & (s >= 0) & (s < 8)


def shifted(values, row, col):
    step = 8 * row + col
    if step == 0:
        return values
    kept = inside(128, row, col)
    pieces = []
    for start in range(0, values.shape[1], 128):
        moved = pltpu.roll(values[:, start : start + 128], (-step) % 128, 1)
        pieces.append(jnp.where(kept, moved, jnp.zeros_like(moved)))
    return jnp.concatenate(pieces, 1) if len(pieces) > 1 else pieces[0]


def field_kernel(
    core, reinit, slots, noise, buffer, cotangent, field, keep, send, fresh, stored, cot, act, fresh_at, slot_at, sem
):
    pixels = field.shape[1]
    half = pixels // 2
    lane = lax.broadcasted_iota(jnp.int32, (1, 128), 1)
    sources = (reinit, slots, noise, buffer, cotangent)
    places = (fresh_at, slot_at, fresh, stored, cot)
    copies = [
        pltpu.make_async_copy(source, place, sem.at[at])
        for at, (source, place) in enumerate(zip(sources, places))
    ]
    for copy in copies:
        copy.start()
    for copy in copies:
        copy.wait()

    def place(image, block):
        slot = slot_at[image]
        found = stored[:, pl.ds(pl.multiple_of((slot >> 1) * 128, 128), 128)]
        found = jnp.where((slot & 1) == (image & 1), found, pltpu.roll(found, 64, 1))
        return jnp.where(fresh_at[image] == 1, block, found)

    for pair in range(pixels // 128):
        here = pl.ds(pair * 128, 128)
        block = fresh[:, here]
        value = jnp.where(lane < 64, place(2 * pair, block), place(2 * pair + 1, block))
        field[:, here] = value
        value = value.astype(f32)
        act[:, here] = (value * jax.nn.sigmoid(value)).astype(bf16)

    for at, out in ((core[0], keep), (1 - core[0], send)):
        lanes = pl.ds(pl.multiple_of(at * half, 128), half)
        out[:, :half] = act[:, lanes]
        out[:, half:] = cot[:, lanes]


def place_kernel(core, keep, came, block):
    depth, half = keep.shape[0], block.shape[2]
    for at, part in ((core[0], keep), (1 - core[0], came)):
        block[0, pl.ds(pl.multiple_of(at * depth, 16), depth), :] = part[:, :half]


def write_shifts(stack, values, taps=range(9)):
    depth = values.shape[0]
    for at, tap in enumerate(taps):
        row, col = offsets[tap]
        stack[pl.ds(at * depth, depth), :] = shifted(values, -row, -col)


def back_kernel(start, order, own, other, kernel_own, kernel_other, send, keep, stack_own, stack_other, block):
    half, depth, pixels = keep.shape
    write_shifts(stack_own, own[:, start : start + pixels])
    write_shifts(stack_other, other[:, start : start + pixels])

    def step(at, _):
        lanes = pl.ds(pl.multiple_of(at * TILE, TILE), TILE)
        total = None
        for kernel, stack in ((kernel_own, stack_own), (kernel_other, stack_other)):
            part = lax.dot_general(
                kernel[...], stack[:, lanes], (((0,), (0,)), ((), ())), preferred_element_type=f32
            )
            total = part if total is None else total + part
        block[...] = total
        for slot in range(2 * half):
            rows = block[pl.ds(pl.multiple_of(order[slot] * depth, 8), depth), :]
            if slot < half:
                keep[slot, :, lanes] = rows
            else:
                send[slot - half, :, lanes] = rows.astype(bf16)
        return 0

    lax.fori_loop(0, pixels // TILE, step, 0)


def fetch(order, pieces, whole, sem):
    copies = []
    for piece in pieces:
        for at in range(piece.shape[0]):
            slot, depth = len(copies), piece.shape[1]
            start = pl.multiple_of(order[slot] * depth, 16)
            copies.append(
                pltpu.make_async_copy(piece.at[at], whole.at[pl.ds(start, depth), :], sem.at[slot])
            )
            copies[-1].start()
    return copies


def conv_tile(kernel, tile):
    depth = kernel.shape[0] // 9
    spread = jnp.dot(kernel[...], tile, preferred_element_type=f32)
    total = spread[4 * depth : 5 * depth]
    for tap, (row, col) in enumerate(offsets):
        if tap != 4:
            total = total + shifted(spread[tap * depth : (tap + 1) * depth], row, col)
    return total


def conv_one_kernel(
    core, order, own, near, across, beyond, kernel_own, kernel_other, bias_own, bias_other, whole, pre_own, pre_other, act, sem
):
    for copy in fetch(order, (own, near, across, beyond), whole, sem):
        copy.wait()
    depth = pre_own.shape[0]

    def step(at, _):
        lanes = pl.ds(pl.multiple_of(at * CONV_TILE, CONV_TILE), CONV_TILE)
        tile = whole[:, lanes]
        for kernel, bias, pre, place in (
            (kernel_own, bias_own, pre_own, core[0]),
            (kernel_other, bias_other, pre_other, 1 - core[0]),
        ):
            value = conv_tile(kernel, tile) + bias[:, :1].astype(f32)
            pre[:, lanes] = value
            rows = pl.ds(pl.multiple_of(place * depth, 16), depth)
            act[0, rows, lanes] = (value * jax.nn.sigmoid(value)).astype(bf16)
        return 0

    lax.fori_loop(0, whole.shape[1] // CONV_TILE, step, 0)


def conv_two_kernel(whole, kernel_own, kernel_other, out_own, out_other):
    def step(at, _):
        lanes = pl.ds(pl.multiple_of(at * CONV_TILE, CONV_TILE), CONV_TILE)
        tile = whole[:, lanes]
        out_own[:, lanes] = conv_tile(kernel_own, tile)
        out_other[:, lanes] = conv_tile(kernel_other, tile)
        return 0

    lax.fori_loop(0, whole.shape[1] // CONV_TILE, step, 0)


def slope_kernel(core, kept, near, far, pre_own, pre_other, own, other):
    depth = own.shape[0]
    for pre, place, out in ((pre_own, core[0], own), (pre_other, 1 - core[0], other)):
        rows = pl.ds(pl.multiple_of(place * depth, 16), depth)
        upstream = kept[0, rows, :] + near[0, rows, :].astype(f32) + far[0, rows, :].astype(f32)
        out[...] = (upstream * silu_slope(pre[...])).astype(bf16)


def write_grad(low, taps, parts, outs, grad, stacks):
    transposed = (((1,), (1,)), ((), ()))
    depth = parts[0][0].shape[0]
    rows = len(taps) * depth
    total = sums = None
    for at, (values, whole) in enumerate(parts):
        write_shifts(stacks.at[at], values, taps)
        part = lax.dot_general(stacks[at], whole[...], transposed, preferred_element_type=f32)
        total = part if total is None else total + part
        if taps[-1] == 8:
            ones = jnp.ones((EXTRA, values.shape[1]), bf16)
            part = lax.dot_general(ones, values, transposed, preferred_element_type=f32)
            sums = part if sums is None else sums + part
    grad[:rows, :] = total
    if taps[-1] == 8:
        grad[rows:, :] = jnp.zeros((EXTRA, grad.shape[1]), f32)
        grad[rows:, :depth] = sums
    base = 0
    for send, keep in outs:
        size = keep.shape[0]
        mine = pl.multiple_of(base + low[0] * size, 8)
        theirs = pl.multiple_of(base + (1 - low[0]) * size, 8)
        keep[...] = grad[pl.ds(mine, size), :]
        send[...] = grad[pl.ds(theirs, size), :].astype(bf16)
        base += 2 * size


def grad_one_kernel(taps, low, own, came, whole, whole_came, send, keep, grad, stacks):
    parts = (own[...], whole), (came[...], whole_came)
    write_grad(low, taps, parts, ((send, keep),), grad, stacks)


def grad_two_kernel(low, core, cotangent, whole, whole_came, send, keep_a, keep_b, grad, stacks):
    half = whole.shape[1]
    own, came = (
        cotangent[:, pl.ds(pl.multiple_of(at * half, 128), half)] for at in (core[0], 1 - core[0])
    )
    parts = (own, whole), (came, whole_came)
    size = keep_a.shape[0]
    outs = (send.at[:size], keep_a), (send.at[size:], keep_b)
    write_grad(low, tuple(range(9)), parts, outs, grad, stacks)


def add_split_kernel(keep_a, keep_b, near, out_a, out_b):
    size = keep_a.shape[0]
    out_a[...] = (keep_a[...] + near[:size].astype(f32)).astype(bf16)
    out_b[...] = (keep_b[...] + near[size:].astype(f32)).astype(bf16)


def copy_kernel(*refs):
    for values, out in zip(refs[: len(refs) // 2], refs[len(refs) // 2 :]):
        out[...] = values[...]


def add_kernel(left, right, out):
    out[...] = (left[...].astype(f32) + right[...].astype(f32)).astype(bf16)


def join_kernel(*refs):
    out, base = refs[-1], 0
    for left, right in zip(refs[0:-1:2], refs[1:-1:2]):
        size = left.shape[0]
        out[base : base + size, :] = (left[...].astype(f32) + right[...].astype(f32)).astype(bf16)
        base += size


def assemble_kernel(order, *refs):
    *pieces, whole, sem = refs
    for copy in fetch(order, pieces, whole, sem):
        copy.wait()


def sum_kernel(core, kept, near, far, own, other):
    depth = own.shape[0]
    for place, out in ((core[0], own), (1 - core[0], other)):
        rows = pl.ds(pl.multiple_of(place * depth, 16), depth)
        out[...] = kept[0, rows, :] + near[0, rows, :].astype(f32) + far[0, rows, :].astype(f32)


def output_kernel(core, field, own, came, bias, out, total, sem):
    half = own.shape[1]
    column = bias[:, :1].astype(f32)
    for at, part in ((core[0], own), (1 - core[0], came)):
        lanes = pl.ds(pl.multiple_of(at * half, 128), half)
        total[:, lanes] = (field[:, lanes].astype(f32) + part[...] + column).astype(bf16)
    copy = pltpu.make_async_copy(total, out, sem)
    copy.start()
    copy.wait()


def field_grad_kernel(core, field, cotangent, own, came, out, total, sem):
    half = own.shape[1]
    for at, part in ((core[0], own), (1 - core[0], came)):
        lanes = pl.ds(pl.multiple_of(at * half, 128), half)
        slope = silu_slope(field[:, lanes].astype(f32))
        total[:, lanes] = cotangent[:, lanes].astype(f32) + part[...] * slope
    copy = pltpu.make_async_copy(total, out, sem)
    copy.start()
    copy.wait()


def onward_kernel(keep, near, out):
    out[0] = (keep[1] + near[1].astype(f32)).astype(bf16)


def finish_kernel(sizes, low, *refs):
    pieces, (grad, bias, total, sem) = refs[:-4], refs[-4:]
    for place, side in ((low[0], pieces[0::2]), (1 - low[0], pieces[1::2])):
        rows = [(piece, at) for piece in side for at in range(0, piece.shape[0], 8)]
        base, at = 0, 0
        for size in sizes:
            left = size
            while left:
                piece, inner = rows[at // 8]
                count = min(left, piece.shape[0] - inner)
                start = pl.multiple_of(base + place * size + size - left, 8)
                total[pl.ds(start, count), :] = piece[inner : inner + count, :].astype(f32)
                at += count
                left -= count
            base += 2 * size
    copy = pltpu.make_async_copy(total.at[pl.ds(0, grad.shape[0]), :], grad, sem)
    copy.start()
    bias[...] = total[grad.shape[0] : grad.shape[0] + 1, : bias.shape[1]]
    copy.wait()


SMEM = pl.BlockSpec(memory_space=pltpu.SMEM)
VMEM = pl.BlockSpec(memory_space=pltpu.VMEM)
ANY = pl.BlockSpec(memory_space=pl.ANY)
HBM = pl.BlockSpec(memory_space=pltpu.HBM)
SPACES = {id(VMEM): pltpu.VMEM, id(HBM): pltpu.HBM}


def run(body, name, ins, outs, scratch=(), out_specs=None, after=(), cost=0):
    count, total = len(ins), len(ins) + len(after)
    end = total + len(outs)

    def marked(*refs):
        body(*refs[:count], *refs[total:end], *refs[end + 1 :])
        refs[end][...] = jnp.zeros_like(refs[end])

    ins = list(ins) + [(VMEM, value) for value in after]
    args = [
        pltpu.with_memory_space_constraint(arg, SPACES[id(spec)]) if id(spec) in SPACES else arg
        for spec, arg in ins
    ]
    out_specs = list(out_specs or [VMEM] * len(outs)) + [VMEM]
    outs = list(outs) + [jax.ShapeDtypeStruct((8, 128), f32)]
    return pl.pallas_call(
        marked,
        name=name,
        out_shape=[
            SPACES[id(spec)](out.shape, out.dtype) if id(spec) in SPACES else out
            for spec, out in zip(out_specs, outs)
        ],
        in_specs=[spec for spec, _ in ins],
        out_specs=out_specs,
        scratch_shapes=list(scratch),
        cost_estimate=pl.CostEstimate(flops=cost, bytes_accessed=0, transcendentals=0),
        compiler_params=pltpu.CompilerParams(vmem_limit_bytes=VMEM_LIMIT),
    )(*args)


def split_local(
    groups, width, noise, buffer, reinit, slots, kernel_one, bias_one, kernel_two, bias_two, cotangent
):
    depth, pixels = noise.shape
    channels = kernel_one.shape[2]
    half = pixels // 2
    chips = width // 2
    block = 2 * depth
    rows = 9 * depth
    index = lax.axis_index("blk")
    core = index % 2
    chip = index // 2
    group = lax.axis_index("dp")
    shape = jax.ShapeDtypeStruct
    dma = pltpu.SemaphoreType.DMA

    first = [2, 4]

    def swap(values, axis, pairs, name):
        with jax.named_scope(name):
            return lax.ppermute(values, axis, pairs)

    def chip_swap(values, step, name):
        pairs = [(i, i ^ first[(step + i) % 2]) for i in range(width)]
        return swap(values, "blk", pairs, name)

    def core_swap(values, name):
        return swap(values, "blk", [(i, i ^ 1) for i in range(width)], name)

    def group_swap(values, bit, name):
        return swap(values, "dp", [(i, i ^ bit) for i in range(groups)], name)

    def order_of(which):
        swapped = jnp.where(which == 0, jnp.array([0, 1, 2, 3]), jnp.array([0, 2, 1, 3]))
        return jnp.bitwise_xor(chip, swapped).astype(jnp.int32)

    order, order_came = order_of(core), order_of(1 - core)
    core_at = core.reshape(1).astype(jnp.int32)
    low = (group % 2).reshape(1).astype(jnp.int32)

    def vmem(*values):
        return [(VMEM, value) for value in values]

    def like(*values):
        return [shape(value.shape, bf16) for value in values]

    own_one = kernel_one.reshape(rows, channels)
    own_two = kernel_two.reshape(rows, channels)
    other_two = core_swap(own_two, "kernel_two")
    other_one = core_swap(own_one, "kernel_one")
    bias_own = jnp.broadcast_to(bias_one[:, None], (depth, 128))
    bias_other = core_swap(bias_own, "bias")

    marks, costs = [], [EARLY, "place", "copy", "add", "join", "onward", "sum", "assemble", EARLY]

    def step(body, name, ins, outs, scratch=(), out_specs=None):
        *results, mark = run(body, name, ins, outs, scratch, out_specs, marks[-1:], costs[-1][name in costs])
        marks.append(mark)
        return results[0] if len(results) == 1 else results

    part = shape((depth, half), bf16)
    piece = shape((1, block, half), bf16)
    wide = shape((depth, pixels), bf16)
    field, keep, send = step(
        field_kernel,
        "field",
        [(SMEM, core_at)] + [(HBM, v) for v in (reinit, slots, noise, buffer, cotangent)],
        [wide, wide, wide],
        [
            pltpu.VMEM(noise.shape, bf16),
            pltpu.VMEM(buffer.shape, bf16),
            pltpu.VMEM(cotangent.shape, bf16),
            pltpu.VMEM(noise.shape, bf16),
            pltpu.SMEM(reinit.shape, jnp.int32),
            pltpu.SMEM(slots.shape, jnp.int32),
            dma((5,)),
        ],
    )
    came = core_swap(send, "pair")
    zero = step(place_kernel, "place", [(SMEM, core_at)] + vmem(keep, came), [piece])
    zero_near, zero_across = chip_swap(zero, 0, "zero_near"), chip_swap(zero, 1, "zero_across")

    def back(name, start, own, other, kernel_own, kernel_other):
        return step(
            functools.partial(back_kernel, start),
            name,
            [(SMEM, order)] + vmem(own, other, kernel_own, kernel_other),
            [
                shape((chips // 2, block, half), bf16),
                shape((chips // 2, block, half), f32),
            ],
            [
                pltpu.VMEM((rows, half), bf16),
                pltpu.VMEM((rows, half), bf16),
                pltpu.VMEM((channels, TILE), f32),
            ],
        )

    send, keep_two = back("back_two", half, keep, came, own_two, other_two)
    zero_near, zero_across = step(
        copy_kernel, "copy", vmem(zero_near, zero_across), like(zero_near, zero_across)
    )
    zero_beyond = chip_swap(zero_near, 1, "zero_beyond")
    send, field = step(copy_kernel, "copy", vmem(send, field), like(send, field))
    near_two = chip_swap(send, 1, "two_near")

    whole = shape((channels, half), bf16)
    plane = shape((depth, half), f32)
    whole_zero, pre_own, pre_other, one = step(
        conv_one_kernel,
        "conv_one",
        [(SMEM, core_at), (SMEM, order)]
        + vmem(zero, zero_near, zero_across, zero_beyond)
        + vmem(own_one, other_one, bias_own, bias_other),
        [whole, plane, plane, piece],
        [dma((chips,))],
    )
    whole_zero_came = core_swap(whole_zero, "zero_pair")
    onward = step(onward_kernel, "onward", vmem(keep_two, near_two), [piece])
    far_two = chip_swap(onward, 0, "two_far")

    pre_grad, pre_grad_send = step(
        slope_kernel,
        "slope",
        [(SMEM, core_at)] + vmem(keep_two, near_two, far_two, pre_own, pre_other),
        [part, part],
    )
    pre_grad_came = core_swap(pre_grad_send, "pre_grad")
    one = step(copy_kernel, "copy", vmem(one), like(one))
    one_near, one_across = chip_swap(one, 0, "one_near"), chip_swap(one, 1, "one_across")

    chunks = (tuple(range(SPLIT)), tuple(range(SPLIT, 9)))
    sizes = [SPLIT * depth // 2, ((9 - SPLIT) * depth + EXTRA) // 2]

    def grad_outs(size):
        return [shape((size, channels), bf16), shape((size, channels), f32)]

    def grad_scratch(taps):
        extra = EXTRA if taps[-1] == 8 else 0
        return [
            pltpu.VMEM((len(taps) * depth + extra, channels), f32),
            pltpu.VMEM((2, len(taps) * depth, half), bf16),
        ]

    costs[-1] = LATE
    grads = []
    for at, taps in enumerate(chunks):
        send, keep = step(
            functools.partial(grad_one_kernel, taps),
            "grad_one_" + "ab"[at],
            [(SMEM, low)] + vmem(pre_grad, pre_grad_came, whole_zero, whole_zero_came),
            grad_outs(sizes[at]),
            grad_scratch(taps),
        )
        grads.append((keep, group_swap(send, 1, "one_A" + "ab"[at])))

    one_near, one_across, pre_grad, pre_grad_send = step(
        copy_kernel,
        "copy",
        vmem(one_near, one_across, pre_grad, pre_grad_send),
        like(one_near, one_across, pre_grad, pre_grad_send),
    )
    one_beyond = chip_swap(one_near, 1, "one_beyond")
    mine_a = step(add_kernel, "add", vmem(*grads[0]), like(grads[0][1]))
    far_a = group_swap(mine_a, 2, "one_Ba")
    mine_b = step(add_kernel, "add", vmem(*grads[1]), like(grads[1][1]))
    far_b = group_swap(mine_b, 2, "one_Bb")

    whole_one = step(
        assemble_kernel,
        "assemble",
        [(SMEM, order)] + vmem(one, one_near, one_across, one_beyond),
        [whole],
        [dma((chips,))],
    )
    whole_one_came = core_swap(whole_one, "one_pair")
    out_own, out_other = step(
        conv_two_kernel, "conv_two", vmem(whole_one, own_two, other_two), [plane, plane]
    )
    out_came = core_swap(out_other, "out_pair")

    size = sum(sizes)
    send, keep_a, keep_b = step(
        grad_two_kernel,
        "grad_two",
        [(SMEM, low), (SMEM, core_at)] + vmem(cotangent, whole_one, whole_one_came),
        [shape((size, channels), bf16)] + [shape((count, channels), f32) for count in sizes],
        grad_scratch(tuple(range(9))),
    )
    near = group_swap(send, 1, "two_A")
    output = step(
        output_kernel,
        "output",
        [(SMEM, core_at)]
        + vmem(field, out_own, out_came, jnp.broadcast_to(bias_two[:, None], (depth, 128))),
        [wide],
        [pltpu.VMEM((depth, pixels), bf16), dma],
        out_specs=[ANY],
    )

    send, keep_one = back("back_one", 0, pre_grad, pre_grad_send, own_one, other_one)
    near_one = chip_swap(send, 1, "one_near")

    half_one = step(
        join_kernel, "join", vmem(mine_a, far_a, mine_b, far_b), [shape((size, channels), bf16)]
    )
    rest_one = group_swap(half_one, 1, "one_C")
    mine_a, mine_b = step(
        add_split_kernel,
        "add",
        vmem(keep_a, keep_b, near),
        [shape((count, channels), bf16) for count in sizes],
    )
    far_a = group_swap(mine_a, 2, "two_Ba")
    far_b = group_swap(mine_b, 2, "two_Bb")

    def finish(name, pieces):
        kernel_grad, bias_grad = step(
            functools.partial(finish_kernel, sizes),
            name,
            [(SMEM, low)] + vmem(*pieces),
            [shape((rows, channels), f32), shape((1, depth), f32)],
            [pltpu.VMEM((rows + EXTRA, channels), f32), dma],
            out_specs=[ANY, VMEM],
        )
        return kernel_grad.reshape(9, depth, channels), bias_grad.reshape(depth)

    onward = step(onward_kernel, "onward", vmem(keep_one, near_one), [piece])
    far_one = chip_swap(onward, 0, "one_far")
    kernel_grad_one, bias_grad_one = finish("finish_one", [half_one, rest_one])
    own, other = step(
        sum_kernel, "sum", [(SMEM, core_at)] + vmem(keep_one, near_one, far_one), [plane, plane]
    )
    other = core_swap(other, "field_pair")

    half_a = step(add_kernel, "add", vmem(mine_a, far_a), like(mine_a))
    rest_a = group_swap(half_a, 1, "two_Ca")
    half_b = step(add_kernel, "add", vmem(mine_b, far_b), like(mine_b))
    rest_b = group_swap(half_b, 1, "two_Cb")
    grad_field = step(
        field_grad_kernel,
        "field_grad",
        [(SMEM, core_at)] + vmem(field, cotangent, own, other),
        [shape((depth, pixels), f32)],
        [pltpu.VMEM((depth, pixels), f32), dma],
        out_specs=[ANY],
    )
    kernel_grad_two, bias_grad_two = finish("finish_two", [half_a, rest_a, half_b, rest_b])
    return output, grad_field, kernel_grad_one, bias_grad_one, kernel_grad_two, bias_grad_two


def shift_tap(field, row, col):
    depth = field.shape[0]
    grid = field.reshape(depth, -1, 8, 8)
    grid = jnp.pad(grid, ((0, 0), (0, 0), (1, 1), (1, 1)))
    grid = grid[:, :, 1 + row : 9 + row, 1 + col : 9 + col]
    return grid.reshape(depth, -1)


def add_conv(total, piece, kernel):
    for number, (row, col) in enumerate(offsets):
        total = total + jnp.dot(
            kernel[number], shift_tap(piece, row, col), preferred_element_type=f32
        )
    return total


def add_grad(piece, upstream):
    parts = [
        lax.dot_general(
            upstream,
            shift_tap(piece, row, col),
            (((1,), (1,)), ((), ())),
            preferred_element_type=f32,
        )
        for row, col in offsets
    ]
    return jnp.stack(parts, 0)


def back_shifts(upstream):
    return jnp.stack([shift_tap(upstream, -row, -col) for row, col in offsets], 0)


def spread_rows(kernel, moved):
    return lax.dot_general(kernel, moved, (((0, 1), (0, 1)), ((), ())), preferred_element_type=f32)


def plain_local(
    noise, buffer, reinit, slots, kernel_one, bias_one, kernel_two, bias_two, cotangent
):
    depth = noise.shape[0]
    images = reinit.shape[0]
    pixels = images * 64
    stored = buffer.reshape(depth, -1, 64)[:, slots, :]
    fresh = noise.reshape(depth, images, 64)
    field = (
        jnp.where(reinit[None, :, None] == 1, fresh, stored).reshape(depth, pixels).astype(f32)
    )
    act_zero = jax.nn.silu(field).astype(bf16)
    empty = jnp.zeros((depth, pixels), f32)
    whole_zero = lax.all_gather(act_zero, "blk", axis=0, tiled=True)
    pre_one = add_conv(empty, whole_zero, kernel_one)
    pre_one = pre_one + bias_one.astype(f32)[:, None]
    act_one = jax.nn.silu(pre_one).astype(bf16)
    whole_one = lax.all_gather(act_one, "blk", axis=0, tiled=True)
    pre_two = add_conv(empty, whole_one, kernel_two)
    output = (field + pre_two + bias_two.astype(f32)[:, None]).astype(bf16)
    bias_grad_two = jnp.sum(cotangent.astype(f32), axis=1)
    kernel_grad_two = add_grad(whole_one, cotangent)
    grad_act_one = lax.psum_scatter(
        spread_rows(kernel_two, back_shifts(cotangent)), "blk", scatter_dimension=0, tiled=True
    )
    grad_pre_one = (grad_act_one * silu_slope(pre_one)).astype(bf16)
    bias_grad_one = jnp.sum(grad_pre_one.astype(f32), axis=1)
    kernel_grad_one = add_grad(whole_zero, grad_pre_one)
    grad_act_zero = lax.psum_scatter(
        spread_rows(kernel_one, back_shifts(grad_pre_one)).astype(bf16),
        "blk",
        scatter_dimension=0,
        tiled=True,
    ).astype(f32)
    grad_field = cotangent.astype(f32) + grad_act_zero * silu_slope(field)
    summed = lax.psum((kernel_grad_one, bias_grad_one, kernel_grad_two, bias_grad_two), "dp")
    return (output, grad_field, summed[0], summed[1], summed[2], summed[3])


def solution(mesh):
    groups, width = mesh.shape["dp"], mesh.shape["blk"]

    def local(noise, *rest):
        if groups == 4 and width == 8 and noise.shape[0] % 16 == 0 and noise.shape[1] % 512 == 0:
            return split_local(groups, width, noise, *rest)
        return plain_local(noise, *rest)

    return jax.shard_map(
        local,
        mesh=mesh,
        in_specs=(
            P("blk", "dp"),
            P("blk", "dp"),
            P("dp"),
            P("dp"),
            P(None, "blk", None),
            P("blk"),
            P(None, "blk", None),
            P("blk"),
            P("blk", "dp"),
        ),
        out_specs=(
            P("blk", "dp"),
            P("blk", "dp"),
            P(None, "blk", None),
            P("blk"),
            P(None, "blk", None),
            P("blk"),
        ),
        check_vma=False,
    )
```

```python
import functools

import jax
import jax.numpy as jnp
from jax import lax
from jax.experimental import pallas as pl
from jax.experimental.pallas import tpu as pltpu
from jax.sharding import PartitionSpec as P

bf16 = jnp.bfloat16
f32 = jnp.float32
offsets = [(row, col) for row in (-1, 0, 1) for col in (-1, 0, 1)]
VMEM_LIMIT = 20 << 20
COSTS = {
    "early": {"big": 10**10, "small": 0},
    "late": {"big": 2 * 10**10, "small": 10**9},
}
SMALL = ("place", "copy", "add", "join", "onward", "sum", "assemble")
EXTRA = 16
PARTS_ONE, PARTS_TWO = (4, 9), (5, 9)
TILE = 256
CONV_TILE = 512


def silu_slope(value):
    sigma = jax.nn.sigmoid(value)
    return sigma * (1.0 + value * (1.0 - sigma))


def inside(width, row, col):
    pixel = lax.broadcasted_iota(jnp.int32, (1, width), 1)
    r = ((pixel >> 3) & 7) + row
    s = (pixel & 7) + col
    return (r >= 0) & (r < 8) & (s >= 0) & (s < 8)


def shifted(values, row, col):
    step = 8 * row + col
    if step == 0:
        return values
    kept = inside(128, row, col)
    pieces = []
    for start in range(0, values.shape[1], 128):
        moved = pltpu.roll(values[:, start : start + 128], (-step) % 128, 1)
        pieces.append(jnp.where(kept, moved, jnp.zeros_like(moved)))
    return jnp.concatenate(pieces, 1) if len(pieces) > 1 else pieces[0]


def field_kernel(
    core, reinit, slots, noise, buffer, cotangent, field, keep, send, fresh, stored, cot, act, fresh_at, slot_at, sem
):
    pixels = field.shape[1]
    half = pixels // 2
    lane = lax.broadcasted_iota(jnp.int32, (1, 128), 1)
    sources = (reinit, slots, noise, buffer, cotangent)
    places = (fresh_at, slot_at, fresh, stored, cot)
    copies = [
        pltpu.make_async_copy(source, place, sem.at[at])
        for at, (source, place) in enumerate(zip(sources, places))
    ]
    for copy in copies:
        copy.start()
    for copy in copies:
        copy.wait()

    def place(image, block):
        slot = slot_at[image]
        found = stored[:, pl.ds(pl.multiple_of((slot >> 1) * 128, 128), 128)]
        found = jnp.where((slot & 1) == (image & 1), found, pltpu.roll(found, 64, 1))
        return jnp.where(fresh_at[image] == 1, block, found)

    for pair in range(pixels // 128):
        here = pl.ds(pair * 128, 128)
        block = fresh[:, here]
        value = jnp.where(lane < 64, place(2 * pair, block), place(2 * pair + 1, block))
        field[:, here] = value
        value = value.astype(f32)
        act[:, here] = (value * jax.nn.sigmoid(value)).astype(bf16)

    for at, out in ((core[0], keep), (1 - core[0], send)):
        lanes = pl.ds(pl.multiple_of(at * half, 128), half)
        out[:, :half] = act[:, lanes]
        out[:, half:] = cot[:, lanes]


def place_kernel(core, keep, came, block):
    depth, half = keep.shape[0], block.shape[2]
    for at, part in ((core[0], keep), (1 - core[0], came)):
        block[0, pl.ds(pl.multiple_of(at * depth, 16), depth), :] = part[:, :half]


def write_shifts(stack, values, taps=range(9)):
    depth = values.shape[0]
    for at, tap in enumerate(taps):
        row, col = offsets[tap]
        stack[pl.ds(at * depth, depth), :] = shifted(values, -row, -col)


def back_kernel(start, order, own, other, kernel_own, kernel_other, *refs):
    *sends, keep, stack_own, stack_other, block, held, sem = refs
    copy = pltpu.make_async_copy(kernel_own, held, sem)
    copy.start()
    half, depth, pixels = keep.shape
    places = [send.at[at] for send in sends for at in range(send.shape[0])]
    write_shifts(stack_own, own[:, start : start + pixels])
    write_shifts(stack_other, other[:, start : start + pixels])
    copy.wait()

    def step(at, _):
        lanes = pl.ds(pl.multiple_of(at * TILE, TILE), TILE)
        total = None
        for kernel, stack in ((held, stack_own), (kernel_other, stack_other)):
            part = lax.dot_general(
                kernel[...], stack[:, lanes], (((0,), (0,)), ((), ())), preferred_element_type=f32
            )
            total = part if total is None else total + part
        block[...] = total
        for slot in range(2 * half):
            rows = block[pl.ds(pl.multiple_of(order[slot] * depth, 8), depth), :]
            if slot < half:
                keep[slot, :, lanes] = rows
            else:
                places[slot - half][:, lanes] = rows.astype(bf16)
        return 0

    lax.fori_loop(0, pixels // TILE, step, 0)


def fetch(order, pieces, whole, sem):
    copies = []
    for piece in pieces:
        for at in range(piece.shape[0]):
            slot, depth = len(copies), piece.shape[1]
            start = pl.multiple_of(order[slot] * depth, 16)
            copies.append(
                pltpu.make_async_copy(piece.at[at], whole.at[pl.ds(start, depth), :], sem.at[slot])
            )
            copies[-1].start()
    return copies


def conv_tile(kernel, tile):
    depth = kernel.shape[0] // 9
    spread = jnp.dot(kernel[...], tile, preferred_element_type=f32)
    total = spread[4 * depth : 5 * depth]
    for tap, (row, col) in enumerate(offsets):
        if tap != 4:
            total = total + shifted(spread[tap * depth : (tap + 1) * depth], row, col)
    return total


def conv_one_kernel(
    core, order, three, beyond, kernel_own, kernel_other, bias_own, bias_other, whole, pre_own, pre_other, act, sem
):
    for copy in fetch(order, (three, beyond), whole, sem):
        copy.wait()
    depth = pre_own.shape[0]

    def step(at, _):
        lanes = pl.ds(pl.multiple_of(at * CONV_TILE, CONV_TILE), CONV_TILE)
        tile = whole[:, lanes]
        for kernel, bias, pre, place in (
            (kernel_own, bias_own, pre_own, core[0]),
            (kernel_other, bias_other, pre_other, 1 - core[0]),
        ):
            value = conv_tile(kernel, tile) + bias[:, :1].astype(f32)
            pre[:, lanes] = value
            rows = pl.ds(pl.multiple_of(place * depth, 16), depth)
            act[0, rows, lanes] = (value * jax.nn.sigmoid(value)).astype(bf16)
        return 0

    lax.fori_loop(0, whole.shape[1] // CONV_TILE, step, 0)


def conv_two_kernel(whole, kernel_own, kernel_other, out_own, out_other):
    def step(at, _):
        lanes = pl.ds(pl.multiple_of(at * CONV_TILE, CONV_TILE), CONV_TILE)
        tile = whole[:, lanes]
        out_own[:, lanes] = conv_tile(kernel_own, tile)
        out_other[:, lanes] = conv_tile(kernel_other, tile)
        return 0

    lax.fori_loop(0, whole.shape[1] // CONV_TILE, step, 0)


def slope_kernel(core, kept, near, far, pre_own, pre_other, own, other):
    depth = own.shape[0]
    for pre, place, out in ((pre_own, core[0], own), (pre_other, 1 - core[0], other)):
        rows = pl.ds(pl.multiple_of(place * depth, 16), depth)
        upstream = kept[0, rows, :] + near[0, rows, :].astype(f32) + far[0, rows, :].astype(f32)
        out[...] = (upstream * silu_slope(pre[...])).astype(bf16)


def write_grad(taps, parts, outs, grad, stacks):
    transposed = (((1,), (1,)), ((), ()))
    depth = parts[0][0].shape[0]
    rows = len(taps) * depth
    total = sums = None
    for at, (values, whole) in enumerate(parts):
        write_shifts(stacks.at[at], values, taps)
        part = lax.dot_general(stacks[at], whole[...], transposed, preferred_element_type=f32)
        total = part if total is None else total + part
        if taps[-1] == 8:
            ones = jnp.ones((EXTRA, values.shape[1]), bf16)
            part = lax.dot_general(ones, values, transposed, preferred_element_type=f32)
            sums = part if sums is None else sums + part
    grad[:rows, :] = total
    if taps[-1] == 8:
        grad[rows:, :] = jnp.zeros((EXTRA, grad.shape[1]), f32)
        grad[rows:, :depth] = sums
    base = 0
    for send, keep in outs:
        size = keep.shape[0]
        keep[...] = grad[base : base + size, :]
        send[...] = grad[base : base + size, :].astype(bf16)
        base += size


def grad_one_kernel(taps, own, came, whole, whole_came, send, keep, grad, stacks):
    parts = (own[...], whole), (came[...], whole_came)
    write_grad(taps, parts, ((send, keep),), grad, stacks)


def grad_two_kernel(core, cotangent, whole, whole_came, *refs):
    *outs, grad, stacks = refs
    half = whole.shape[1]
    own, came = (
        cotangent[:, pl.ds(pl.multiple_of(at * half, 128), half)] for at in (core[0], 1 - core[0])
    )
    parts = (own, whole), (came, whole_came)
    write_grad(tuple(range(9)), parts, list(zip(outs[0::2], outs[1::2])), grad, stacks)


def copy_kernel(*refs):
    for values, out in zip(refs[: len(refs) // 2], refs[len(refs) // 2 :]):
        out[...] = values[...]


def add_kernel(left, right, out):
    out[...] = (left[...].astype(f32) + right[...].astype(f32)).astype(bf16)


def join_kernel(own, near, across, send, field, joined, *outs):
    for at, block in enumerate((own, near, across)):
        joined[at] = block[0]
    for values, out in zip((near, send, field), outs):
        out[...] = values[...]


def assemble_kernel(order, *refs):
    *pieces, whole, sem = refs
    for copy in fetch(order, pieces, whole, sem):
        copy.wait()


def sum_kernel(core, kept, near, far, own, other):
    depth = own.shape[0]
    for place, out in ((core[0], own), (1 - core[0], other)):
        rows = pl.ds(pl.multiple_of(place * depth, 16), depth)
        out[...] = kept[0, rows, :] + near[0, rows, :].astype(f32) + far[0, rows, :].astype(f32)


def output_kernel(core, field, own, came, bias, out, total, sem):
    half = own.shape[1]
    column = bias[:, :1].astype(f32)
    for at, part in ((core[0], own), (1 - core[0], came)):
        lanes = pl.ds(pl.multiple_of(at * half, 128), half)
        total[:, lanes] = (field[:, lanes].astype(f32) + part[...] + column).astype(bf16)
    copy = pltpu.make_async_copy(total, out, sem)
    copy.start()
    copy.wait()


def field_grad_kernel(core, field, cotangent, own, came, out, total, sem):
    half = own.shape[1]
    for at, part in ((core[0], own), (1 - core[0], came)):
        lanes = pl.ds(pl.multiple_of(at * half, 128), half)
        slope = silu_slope(field[:, lanes].astype(f32))
        total[:, lanes] = cotangent[:, lanes].astype(f32) + part[...] * slope
    copy = pltpu.make_async_copy(total, out, sem)
    copy.start()
    copy.wait()


def onward_kernel(keep, near, out):
    out[0] = (keep[1] + near[near.shape[0] - 1].astype(f32)).astype(bf16)


def finish_kernel(inner, *refs):
    pieces, (grad, bias, total, sem) = refs[:-4], refs[-4:]
    base, copies, rows = 0, [], grad.shape[0]
    for at, (made, came) in enumerate(zip(pieces[0::2], pieces[1::2])):
        size = made.shape[0]
        value = jnp.where(inner[0] == 1, made[...], came[...])
        total[base : base + size, :] = value.astype(f32)
        span = pl.ds(base, min(size, rows - base))
        copies.append(pltpu.make_async_copy(total.at[span, :], grad.at[span, :], sem.at[at]))
        copies[-1].start()
        base += size
    bias[...] = total[rows : rows + 1, : bias.shape[1]]
    for copy in copies:
        copy.wait()


SMEM = pl.BlockSpec(memory_space=pltpu.SMEM)
VMEM = pl.BlockSpec(memory_space=pltpu.VMEM)
ANY = pl.BlockSpec(memory_space=pl.ANY)
HBM = pl.BlockSpec(memory_space=pltpu.HBM)
SPACES = {id(VMEM): pltpu.VMEM, id(HBM): pltpu.HBM}


def in_hbm(values):
    return pltpu.with_memory_space_constraint(values, pltpu.HBM)


def run(body, name, ins, outs, scratch=(), out_specs=None, after=(), cost=0):
    count, total = len(ins), len(ins) + len(after)
    end = total + len(outs)

    def marked(*refs):
        body(*refs[:count], *refs[total:end], *refs[end + 1 :])
        refs[end][...] = jnp.zeros_like(refs[end])

    ins = list(ins) + [(VMEM, value) for value in after]
    args = [
        pltpu.with_memory_space_constraint(arg, SPACES[id(spec)]) if id(spec) in SPACES else arg
        for spec, arg in ins
    ]
    out_specs = list(out_specs or [VMEM] * len(outs)) + [VMEM]
    outs = list(outs) + [jax.ShapeDtypeStruct((8, 128), f32)]
    return pl.pallas_call(
        marked,
        name=name,
        out_shape=[
            SPACES[id(spec)](out.shape, out.dtype) if id(spec) in SPACES else out
            for spec, out in zip(out_specs, outs)
        ],
        in_specs=[spec for spec, _ in ins],
        out_specs=out_specs,
        scratch_shapes=list(scratch),
        cost_estimate=pl.CostEstimate(flops=cost, bytes_accessed=0, transcendentals=0),
        compiler_params=pltpu.CompilerParams(vmem_limit_bytes=VMEM_LIMIT),
    )(*args)


def split_local(
    groups, width, noise, buffer, reinit, slots, kernel_one, bias_one, kernel_two, bias_two, cotangent
):
    depth, pixels = noise.shape
    channels = kernel_one.shape[2]
    half = pixels // 2
    chips = width // 2
    block = 2 * depth
    rows = 9 * depth
    index = lax.axis_index("blk")
    core = index % 2
    chip = index // 2
    group = lax.axis_index("dp")
    shape = jax.ShapeDtypeStruct
    dma = pltpu.SemaphoreType.DMA

    first = [2, 4]

    def swap(values, axis, pairs, name):
        with jax.named_scope(name):
            return lax.ppermute(values, axis, pairs)

    def chip_swap(values, step, name):
        pairs = [(i, i ^ first[(step + i) % 2]) for i in range(width)]
        return swap(values, "blk", pairs, name)

    def core_swap(values, name):
        return swap(values, "blk", [(i, i ^ 1) for i in range(width)], name)

    line = {"in": [(0, 1), (3, 2)], "middle": [(1, 2), (2, 1)], "out": [(1, 0), (2, 3)]}

    def group_send(values, way, name):
        return swap(values, "dp", line[way], name + "_" + way)

    def order_of(which):
        swapped = jnp.where(which == 0, jnp.array([0, 1, 2, 3]), jnp.array([0, 2, 1, 3]))
        return jnp.bitwise_xor(chip, swapped).astype(jnp.int32)

    order, order_came = order_of(core), order_of(1 - core)
    core_at = core.reshape(1).astype(jnp.int32)
    inner = ((group == 1) | (group == 2)).reshape(1).astype(jnp.int32)

    def vmem(*values):
        return [(VMEM, value) for value in values]

    def like(*values):
        return [shape(value.shape, bf16) for value in values]

    own_one = kernel_one.reshape(rows, channels)
    own_two = kernel_two.reshape(rows, channels)
    other_two = core_swap(own_two, "kernel_two")
    other_one = core_swap(own_one, "kernel_one")
    bias_own = jnp.broadcast_to(bias_one[:, None], (depth, 128))
    bias_other = core_swap(bias_own, "bias")

    marks, phase = [], ["early"]

    def step(body, name, ins, outs, scratch=(), out_specs=None, also=()):
        after = marks[-1:] + list(also)
        costs = COSTS[phase[0]]
        cost = costs.get(name, costs["small" if name in SMALL else "big"])
        *results, mark = run(body, name, ins, outs, scratch, out_specs, after, cost)
        marks.append(mark)
        return results[0] if len(results) == 1 else results

    part = shape((depth, half), bf16)
    piece = shape((1, block, half), bf16)
    wide = shape((depth, pixels), bf16)
    field, keep, send = step(
        field_kernel,
        "field",
        [(SMEM, core_at)] + [(HBM, v) for v in (reinit, slots, noise, buffer, cotangent)],
        [wide, wide, wide],
        [
            pltpu.VMEM(noise.shape, bf16),
            pltpu.VMEM(buffer.shape, bf16),
            pltpu.VMEM(cotangent.shape, bf16),
            pltpu.VMEM(noise.shape, bf16),
            pltpu.SMEM(reinit.shape, jnp.int32),
            pltpu.SMEM(slots.shape, jnp.int32),
            dma((5,)),
        ],
    )
    came = core_swap(send, "pair")
    zero = step(place_kernel, "place", [(SMEM, core_at)] + vmem(keep, came), [piece])
    zero_near, zero_across = chip_swap(zero, 0, "zero_near"), chip_swap(zero, 1, "zero_across")

    def back(name, start, sends, *values):
        return step(
            functools.partial(back_kernel, start),
            name,
            [(SMEM, order)]
            + vmem(*values[:2])
            + [(HBM, in_hbm(values[2])), (VMEM, values[3])],
            [shape((count, block, half), bf16) for count in sends]
            + [shape((chips // 2, block, half), f32)],
            [
                pltpu.VMEM((rows, half), bf16),
                pltpu.VMEM((rows, half), bf16),
                pltpu.VMEM((channels, TILE), f32),
                pltpu.VMEM((rows, channels), bf16),
                dma,
            ],
        )

    send, last, keep_two = back("back_two", half, (1, 1), keep, came, own_two, other_two)
    last_two = chip_swap(last, 1, "two_last")
    zero, zero_near, send, field = step(
        join_kernel,
        "join",
        vmem(zero, zero_near, zero_across, send, field),
        [shape((3, block, half), bf16)] + like(zero_near, send, field),
        also=[other_one, bias_other],
    )
    zero_beyond = chip_swap(zero_near, 1, "zero_beyond")
    zero_came = core_swap(zero, "zero_pair")
    onward = step(onward_kernel, "onward", vmem(keep_two, last_two), [piece])
    far_two = chip_swap(onward, 0, "two_far")
    send = step(copy_kernel, "copy", vmem(send), like(send))
    near_two = chip_swap(send, 1, "two_near")
    zero_beyond = step(copy_kernel, "copy", vmem(zero_beyond), like(zero_beyond))
    beyond_came = core_swap(zero_beyond, "zero_pair_beyond")

    whole = shape((channels, half), bf16)
    plane = shape((depth, half), f32)
    whole_zero, pre_own, pre_other, one = step(
        conv_one_kernel,
        "conv_one",
        [(SMEM, core_at), (SMEM, order)]
        + vmem(zero, zero_beyond)
        + vmem(own_one, other_one, bias_own, bias_other),
        [whole, plane, plane, piece],
        [dma((chips,))],
    )
    whole_zero_came = step(
        assemble_kernel,
        "assemble",
        [(SMEM, order_came)] + vmem(zero_came, beyond_came),
        [whole],
        [dma((chips,))],
    )

    pre_grad, pre_grad_send = step(
        slope_kernel,
        "slope",
        [(SMEM, core_at)] + vmem(keep_two, near_two, far_two, pre_own, pre_other),
        [part, part],
    )
    pre_grad_came = core_swap(pre_grad_send, "pre_grad")
    one = step(copy_kernel, "copy", vmem(one), like(one))
    one_near, one_across = chip_swap(one, 0, "one_near"), chip_swap(one, 1, "one_across")

    def sizes(taps):
        return len(taps) * depth + (EXTRA if taps[-1] == 8 else 0)

    def grad_outs(taps):
        return [shape((sizes(taps), channels), bf16), shape((sizes(taps), channels), f32)]

    def grad_scratch(taps):
        return [
            pltpu.VMEM((sizes(taps), channels), f32),
            pltpu.VMEM((2, len(taps) * depth, half), bf16),
        ]

    def parts(ends):
        return [tuple(range(start, end)) for start, end in zip((0,) + ends[:-1], ends)]

    def add(left, right):
        return step(add_kernel, "add", vmem(left, right), like(left))

    phase[0] = "late"
    grads = []
    for at, taps in enumerate(parts(PARTS_ONE)):
        send, keep = step(
            functools.partial(grad_one_kernel, taps),
            "grad_one_" + "ab"[at],
            vmem(pre_grad, pre_grad_came, whole_zero, whole_zero_came),
            grad_outs(taps),
            grad_scratch(taps),
        )
        grads.append((send, keep))
    near_a = group_send(grads[0][0], "in", "one_a")
    one_near, one_across, pre_grad, pre_grad_send = step(
        copy_kernel,
        "copy",
        vmem(one_near, one_across, pre_grad, pre_grad_send),
        like(one_near, one_across, pre_grad, pre_grad_send),
    )
    one_beyond = chip_swap(one_near, 1, "one_beyond")

    send, keep_one = back("back_one", 0, (2,), pre_grad, pre_grad_send, own_one, other_one)
    send_one = send
    send_b = step(copy_kernel, "copy", vmem(grads[1][0]), like(grads[1][0]))
    near_b = group_send(send_b, "in", "one_b")
    mine_a = add(grads[0][1], near_a)
    far_a = group_send(mine_a, "middle", "one_a")

    whole_one = step(
        assemble_kernel,
        "assemble",
        [(SMEM, order)] + vmem(one, one_near, one_across, one_beyond),
        [whole],
        [dma((chips,))],
    )
    whole_one_came = core_swap(whole_one, "one_pair")
    send_a, keep_a, send_b, keep_b = step(
        grad_two_kernel,
        "grad_two",
        [(SMEM, core_at)] + vmem(cotangent, whole_one, whole_one_came),
        [out for taps in parts(PARTS_TWO) for out in grad_outs(taps)],
        grad_scratch(tuple(range(9))),
    )
    near_a = group_send(send_a, "in", "two_a")
    send_one = step(copy_kernel, "copy", vmem(send_one), like(send_one))
    near_one = chip_swap(send_one, 1, "one_near")
    out_own, out_other = step(
        conv_two_kernel, "conv_two", vmem(whole_one, own_two, other_two), [plane, plane]
    )
    mine_b = add(grads[1][1], near_b)
    far_b = group_send(mine_b, "middle", "one_b")
    onward = step(onward_kernel, "onward", vmem(keep_one, near_one), [piece])
    half_a = add(mine_a, far_a)
    rest_a = group_send(half_a, "out", "one_a")
    send_b = step(copy_kernel, "copy", vmem(send_b), like(send_b))
    near_b = group_send(send_b, "in", "two_b")
    mine_two_a = add(keep_a, near_a)
    far_two_a = group_send(mine_two_a, "middle", "two_a")
    half_b = add(mine_b, far_b)
    rest_b = group_send(half_b, "out", "one_b")
    rest_a = step(copy_kernel, "copy", vmem(rest_a), like(rest_a))
    mine_two_b = add(keep_b, near_b)
    far_two_b = group_send(mine_two_b, "middle", "two_b")
    onward = step(copy_kernel, "copy", vmem(onward), like(onward))
    far_one = chip_swap(onward, 0, "one_far")
    half_two_a = add(mine_two_a, far_two_a)
    rest_two_a = group_send(half_two_a, "out", "two_a")

    def finish(name, pieces):
        kernel_grad, bias_grad = step(
            finish_kernel,
            name,
            [(SMEM, inner)] + vmem(*pieces),
            [shape((rows, channels), f32), shape((1, depth), f32)],
            [pltpu.VMEM((rows + EXTRA, channels), f32), dma((len(pieces) // 2,))],
            out_specs=[ANY, VMEM],
        )
        return kernel_grad.reshape(9, depth, channels), bias_grad.reshape(depth)

    kernel_grad_one, bias_grad_one = finish("finish_one", [half_a, rest_a, half_b, rest_b])
    out_other = step(copy_kernel, "copy", vmem(out_other), [plane])
    out_came = core_swap(out_other, "out_pair")
    own, other = step(
        sum_kernel, "sum", [(SMEM, core_at)] + vmem(keep_one, near_one, far_one), [plane, plane]
    )
    other = core_swap(other, "field_pair")
    half_two_b = add(mine_two_b, far_two_b)
    rest_two_b = group_send(half_two_b, "out", "two_b")
    rest_two_a = step(copy_kernel, "copy", vmem(rest_two_a), like(rest_two_a))
    output = step(
        output_kernel,
        "output",
        [(SMEM, core_at)]
        + vmem(field, out_own, out_came, jnp.broadcast_to(bias_two[:, None], (depth, 128))),
        [wide],
        [pltpu.VMEM((depth, pixels), bf16), dma],
        out_specs=[ANY],
    )
    grad_field = step(
        field_grad_kernel,
        "field_grad",
        [(SMEM, core_at)] + vmem(field, cotangent, own, other),
        [shape((depth, pixels), f32)],
        [pltpu.VMEM((depth, pixels), f32), dma],
        out_specs=[ANY],
    )
    kernel_grad_two, bias_grad_two = finish(
        "finish_two", [half_two_a, rest_two_a, half_two_b, rest_two_b]
    )
    return output, grad_field, kernel_grad_one, bias_grad_one, kernel_grad_two, bias_grad_two


def shift_tap(field, row, col):
    depth = field.shape[0]
    grid = field.reshape(depth, -1, 8, 8)
    grid = jnp.pad(grid, ((0, 0), (0, 0), (1, 1), (1, 1)))
    grid = grid[:, :, 1 + row : 9 + row, 1 + col : 9 + col]
    return grid.reshape(depth, -1)


def add_conv(total, piece, kernel):
    for number, (row, col) in enumerate(offsets):
        total = total + jnp.dot(
            kernel[number], shift_tap(piece, row, col), preferred_element_type=f32
        )
    return total


def add_grad(piece, upstream):
    parts = [
        lax.dot_general(
            upstream,
            shift_tap(piece, row, col),
            (((1,), (1,)), ((), ())),
            preferred_element_type=f32,
        )
        for row, col in offsets
    ]
    return jnp.stack(parts, 0)


def back_shifts(upstream):
    return jnp.stack([shift_tap(upstream, -row, -col) for row, col in offsets], 0)


def spread_rows(kernel, moved):
    return lax.dot_general(kernel, moved, (((0, 1), (0, 1)), ((), ())), preferred_element_type=f32)


def plain_local(
    noise, buffer, reinit, slots, kernel_one, bias_one, kernel_two, bias_two, cotangent
):
    depth = noise.shape[0]
    images = reinit.shape[0]
    pixels = images * 64
    stored = buffer.reshape(depth, -1, 64)[:, slots, :]
    fresh = noise.reshape(depth, images, 64)
    field = (
        jnp.where(reinit[None, :, None] == 1, fresh, stored).reshape(depth, pixels).astype(f32)
    )
    act_zero = jax.nn.silu(field).astype(bf16)
    empty = jnp.zeros((depth, pixels), f32)
    whole_zero = lax.all_gather(act_zero, "blk", axis=0, tiled=True)
    pre_one = add_conv(empty, whole_zero, kernel_one)
    pre_one = pre_one + bias_one.astype(f32)[:, None]
    act_one = jax.nn.silu(pre_one).astype(bf16)
    whole_one = lax.all_gather(act_one, "blk", axis=0, tiled=True)
    pre_two = add_conv(empty, whole_one, kernel_two)
    output = (field + pre_two + bias_two.astype(f32)[:, None]).astype(bf16)
    bias_grad_two = jnp.sum(cotangent.astype(f32), axis=1)
    kernel_grad_two = add_grad(whole_one, cotangent)
    grad_act_one = lax.psum_scatter(
        spread_rows(kernel_two, back_shifts(cotangent)), "blk", scatter_dimension=0, tiled=True
    )
    grad_pre_one = (grad_act_one * silu_slope(pre_one)).astype(bf16)
    bias_grad_one = jnp.sum(grad_pre_one.astype(f32), axis=1)
    kernel_grad_one = add_grad(whole_zero, grad_pre_one)
    grad_act_zero = lax.psum_scatter(
        spread_rows(kernel_one, back_shifts(grad_pre_one)).astype(bf16),
        "blk",
        scatter_dimension=0,
        tiled=True,
    ).astype(f32)
    grad_field = cotangent.astype(f32) + grad_act_zero * silu_slope(field)
    summed = lax.psum((kernel_grad_one, bias_grad_one, kernel_grad_two, bias_grad_two), "dp")
    return (output, grad_field, summed[0], summed[1], summed[2], summed[3])


def solution(mesh):
    groups, width = mesh.shape["dp"], mesh.shape["blk"]

    def local(noise, *rest):
        if groups == 4 and width == 8 and noise.shape[0] % 16 == 0 and noise.shape[1] % 512 == 0:
            return split_local(groups, width, noise, *rest)
        return plain_local(noise, *rest)

    return jax.shard_map(
        local,
        mesh=mesh,
        in_specs=(
            P("blk", "dp"),
            P("blk", "dp"),
            P("dp"),
            P("dp"),
            P(None, "blk", None),
            P("blk"),
            P(None, "blk", None),
            P("blk"),
            P("blk", "dp"),
        ),
        out_specs=(
            P("blk", "dp"),
            P("blk", "dp"),
            P(None, "blk", None),
            P("blk"),
            P(None, "blk", None),
            P("blk"),
        ),
        check_vma=False,
    )
```

```python
import functools

import jax
import jax.numpy as jnp
from jax import lax
from jax.experimental import pallas as pl
from jax.experimental.pallas import tpu as pltpu
from jax.sharding import PartitionSpec as P

bf16 = jnp.bfloat16
f32 = jnp.float32
offsets = [(row, col) for row in (-1, 0, 1) for col in (-1, 0, 1)]
VMEM_LIMIT = 20 << 20
COSTS = {'early': {'big': 10000000000, 'small': 0, 'slope': 0}, 'late': {'big': 20000000000, 'small': 500000000, 'assemble_one': 30000000000, 'copy': 0, 'add_one_a': 100000000, 'assemble_one_came': 500000000, 'add_one_b': 10000000000, 'copy_6': 1000000000, 'add_one_a_half': 1000000000, 'add_one_b_half': 500000000, 'copy_7': 3000000000, 'back_one': 30000000000, 'conv_two': 100000000, 'grad_one_b': 1000000000, 'copy_beyond_one': 100000000, 'output': 100000000000, 'copy_10': 30000000000, 'field_grad': 10000000000, 'finish_two': 100000000000, 'sum': 1000000000, 'join_one': 30000000000, 'finish_one': 10000000000, 'add_two_a': 1000000000, 'add_two_b_half': 100000000, 'onward_2': 0, 'grad_one_a': 500000000}}
SMALL = ("place", "copy", "add", "join", "onward", "sum", "assemble")
EXTRA = 16
PARTS_ONE, PARTS_TWO = (5, 9), (5, 9)
TILE = 256
CONV_TILE = 512


def silu_slope(value):
    sigma = jax.nn.sigmoid(value)
    return sigma * (1.0 + value * (1.0 - sigma))


def inside(width, row, col):
    pixel = lax.broadcasted_iota(jnp.int32, (1, width), 1)
    r = ((pixel >> 3) & 7) + row
    s = (pixel & 7) + col
    return (r >= 0) & (r < 8) & (s >= 0) & (s < 8)


def shifted(values, row, col):
    step = 8 * row + col
    if step == 0:
        return values
    kept = inside(128, row, col)
    pieces = []
    for start in range(0, values.shape[1], 128):
        moved = pltpu.roll(values[:, start : start + 128], (-step) % 128, 1)
        pieces.append(jnp.where(kept, moved, jnp.zeros_like(moved)))
    return jnp.concatenate(pieces, 1) if len(pieces) > 1 else pieces[0]


def field_kernel(
    core, reinit, slots, noise, buffer, cotangent, field, keep, send, fresh, stored, cot, act, fresh_at, slot_at, sem
):
    pixels = field.shape[1]
    half = pixels // 2
    lane = lax.broadcasted_iota(jnp.int32, (1, 128), 1)
    sources = (reinit, slots, noise, buffer, cotangent)
    places = (fresh_at, slot_at, fresh, stored, cot)
    copies = [
        pltpu.make_async_copy(source, place, sem.at[at])
        for at, (source, place) in enumerate(zip(sources, places))
    ]
    for copy in copies:
        copy.start()
    for copy in copies:
        copy.wait()

    def place(image, block):
        slot = slot_at[image]
        found = stored[:, pl.ds(pl.multiple_of((slot >> 1) * 128, 128), 128)]
        found = jnp.where((slot & 1) == (image & 1), found, pltpu.roll(found, 64, 1))
        return jnp.where(fresh_at[image] == 1, block, found)

    for pair in range(pixels // 128):
        here = pl.ds(pair * 128, 128)
        block = fresh[:, here]
        value = jnp.where(lane < 64, place(2 * pair, block), place(2 * pair + 1, block))
        field[:, here] = value
        value = value.astype(f32)
        act[:, here] = (value * jax.nn.sigmoid(value)).astype(bf16)

    for at, out in ((core[0], keep), (1 - core[0], send)):
        lanes = pl.ds(pl.multiple_of(at * half, 128), half)
        out[:, :half] = act[:, lanes]
        out[:, half:] = cot[:, lanes]


def place_kernel(core, keep, came, block):
    depth, half = keep.shape[0], block.shape[2]
    for at, part in ((core[0], keep), (1 - core[0], came)):
        block[0, pl.ds(pl.multiple_of(at * depth, 16), depth), :] = part[:, :half]


def write_shifts(stack, values, taps=range(9)):
    depth = values.shape[0]
    for at, tap in enumerate(taps):
        row, col = offsets[tap]
        stack[pl.ds(at * depth, depth), :] = shifted(values, -row, -col)


def back_kernel(start, order, own, other, kernel_own, kernel_other, *refs):
    *sends, keep, stack_own, stack_other, block, held, sem = refs
    copy = pltpu.make_async_copy(kernel_own, held, sem)
    copy.start()
    half, depth, pixels = keep.shape
    places = [send.at[at] for send in sends for at in range(send.shape[0])]
    write_shifts(stack_own, own[:, start : start + pixels])
    write_shifts(stack_other, other[:, start : start + pixels])
    copy.wait()

    def step(at, _):
        lanes = pl.ds(pl.multiple_of(at * TILE, TILE), TILE)
        total = None
        for kernel, stack in ((held, stack_own), (kernel_other, stack_other)):
            part = lax.dot_general(
                kernel[...], stack[:, lanes], (((0,), (0,)), ((), ())), preferred_element_type=f32
            )
            total = part if total is None else total + part
        block[...] = total
        for slot in range(2 * half):
            rows = block[pl.ds(pl.multiple_of(order[slot] * depth, 8), depth), :]
            if slot < half:
                keep[slot, :, lanes] = rows
            else:
                places[slot - half][:, lanes] = rows.astype(bf16)
        return 0

    lax.fori_loop(0, pixels // TILE, step, 0)


def fetch(order, pieces, whole, sem):
    copies = []
    for piece in pieces:
        for at in range(piece.shape[0]):
            slot, depth = len(copies), piece.shape[1]
            start = pl.multiple_of(order[slot] * depth, 16)
            copies.append(
                pltpu.make_async_copy(piece.at[at], whole.at[pl.ds(start, depth), :], sem.at[slot])
            )
            copies[-1].start()
    return copies


def conv_tile(kernel, tile):
    depth = kernel.shape[0] // 9
    spread = jnp.dot(kernel[...], tile, preferred_element_type=f32)
    total = spread[4 * depth : 5 * depth]
    for tap, (row, col) in enumerate(offsets):
        if tap != 4:
            total = total + shifted(spread[tap * depth : (tap + 1) * depth], row, col)
    return total


def conv_one_kernel(
    core, order, three, beyond, kernel_own, kernel_other, bias_own, bias_other, whole, pre_own, pre_other, act, sem
):
    for copy in fetch(order, (three, beyond), whole, sem):
        copy.wait()
    depth = pre_own.shape[0]

    def step(at, _):
        lanes = pl.ds(pl.multiple_of(at * CONV_TILE, CONV_TILE), CONV_TILE)
        tile = whole[:, lanes]
        for kernel, bias, pre, place in (
            (kernel_own, bias_own, pre_own, core[0]),
            (kernel_other, bias_other, pre_other, 1 - core[0]),
        ):
            value = conv_tile(kernel, tile) + bias[:, :1].astype(f32)
            pre[:, lanes] = value
            rows = pl.ds(pl.multiple_of(place * depth, 16), depth)
            act[0, rows, lanes] = (value * jax.nn.sigmoid(value)).astype(bf16)
        return 0

    lax.fori_loop(0, whole.shape[1] // CONV_TILE, step, 0)


def conv_two_kernel(whole, kernel_own, kernel_other, out_own, out_other):
    def step(at, _):
        lanes = pl.ds(pl.multiple_of(at * CONV_TILE, CONV_TILE), CONV_TILE)
        tile = whole[:, lanes]
        out_own[:, lanes] = conv_tile(kernel_own, tile)
        out_other[:, lanes] = conv_tile(kernel_other, tile)
        return 0

    lax.fori_loop(0, whole.shape[1] // CONV_TILE, step, 0)


def slope_kernel(core, kept, near, far, pre_own, pre_other, own, other):
    depth = own.shape[0]
    for pre, place, out in ((pre_own, core[0], own), (pre_other, 1 - core[0], other)):
        rows = pl.ds(pl.multiple_of(place * depth, 16), depth)
        upstream = kept[0, rows, :] + near[0, rows, :].astype(f32) + far[0, rows, :].astype(f32)
        out[...] = (upstream * silu_slope(pre[...])).astype(bf16)


def write_grad(taps, parts, outs, grad, stacks):
    transposed = (((1,), (1,)), ((), ()))
    depth = parts[0][0].shape[0]
    rows = len(taps) * depth
    total = sums = None
    for at, (values, whole) in enumerate(parts):
        write_shifts(stacks.at[at], values, taps)
        part = lax.dot_general(stacks[at], whole[...], transposed, preferred_element_type=f32)
        total = part if total is None else total + part
        if taps[-1] == 8:
            ones = jnp.ones((EXTRA, values.shape[1]), bf16)
            part = lax.dot_general(ones, values, transposed, preferred_element_type=f32)
            sums = part if sums is None else sums + part
    grad[:rows, :] = total
    if taps[-1] == 8:
        grad[rows:, :] = jnp.zeros((EXTRA, grad.shape[1]), f32)
        grad[rows:, :depth] = sums
    base = 0
    for out in outs:
        size = out.shape[0]
        out[...] = grad[base : base + size, :].astype(bf16)
        base += size


def grad_one_kernel(taps, own, came, whole, whole_came, out, grad, stacks):
    parts = (own[...], whole), (came[...], whole_came)
    write_grad(taps, parts, (out,), grad, stacks)


def grad_two_kernel(core, cotangent, whole, whole_came, *refs):
    *outs, grad, stacks = refs
    half = whole.shape[1]
    own, came = (
        cotangent[:, pl.ds(pl.multiple_of(at * half, 128), half)] for at in (core[0], 1 - core[0])
    )
    parts = (own, whole), (came, whole_came)
    write_grad(tuple(range(9)), parts, outs, grad, stacks)


def copy_kernel(*refs):
    for values, out in zip(refs[: len(refs) // 2], refs[len(refs) // 2 :]):
        out[...] = values[...]


def add_kernel(left, right, out):
    out[...] = (left[...].astype(f32) + right[...].astype(f32)).astype(bf16)


def join_kernel(own, near, across, *refs):
    others, (joined, *outs) = refs[: len(refs) // 2 - 1], refs[len(refs) // 2 - 1 :]
    for at, block in enumerate((own, near, across)):
        joined[at] = block[0]
    for values, out in zip((near, *others), outs):
        out[...] = values[...]


def assemble_kernel(order, *refs):
    *pieces, whole, sem = refs
    for copy in fetch(order, pieces, whole, sem):
        copy.wait()


def sum_kernel(core, kept, near, far, own, other):
    depth = own.shape[0]
    for place, out in ((core[0], own), (1 - core[0], other)):
        rows = pl.ds(pl.multiple_of(place * depth, 16), depth)
        out[...] = kept[0, rows, :] + near[0, rows, :].astype(f32) + far[0, rows, :].astype(f32)


def output_kernel(core, field, own, came, bias, out, total, sem):
    half = own.shape[1]
    column = bias[:, :1].astype(f32)
    for at, part in ((core[0], own), (1 - core[0], came)):
        lanes = pl.ds(pl.multiple_of(at * half, 128), half)
        total[:, lanes] = (field[:, lanes].astype(f32) + part[...] + column).astype(bf16)
    copy = pltpu.make_async_copy(total, out, sem)
    copy.start()
    copy.wait()


def field_grad_kernel(core, field, cotangent, own, came, out, total, sem):
    half = own.shape[1]
    for at, part in ((core[0], own), (1 - core[0], came)):
        lanes = pl.ds(pl.multiple_of(at * half, 128), half)
        slope = silu_slope(field[:, lanes].astype(f32))
        total[:, lanes] = cotangent[:, lanes].astype(f32) + part[...] * slope
    copy = pltpu.make_async_copy(total, out, sem)
    copy.start()
    copy.wait()


def onward_kernel(keep, near, out):
    out[0] = (keep[1] + near[near.shape[0] - 1].astype(f32)).astype(bf16)


def finish_kernel(inner, *refs):
    pieces, (grad, bias, total, sem) = refs[:-4], refs[-4:]
    base, copies, rows = 0, [], grad.shape[0]
    for at, (made, came) in enumerate(zip(pieces[0::2], pieces[1::2])):
        size = made.shape[0]
        value = jnp.where(inner[0] == 1, made[...], came[...])
        total[base : base + size, :] = value.astype(f32)
        span = pl.ds(base, min(size, rows - base))
        copies.append(pltpu.make_async_copy(total.at[span, :], grad.at[span, :], sem.at[at]))
        copies[-1].start()
        base += size
    bias[...] = total[rows : rows + 1, : bias.shape[1]]
    for copy in copies:
        copy.wait()


SMEM = pl.BlockSpec(memory_space=pltpu.SMEM)
VMEM = pl.BlockSpec(memory_space=pltpu.VMEM)
ANY = pl.BlockSpec(memory_space=pl.ANY)
HBM = pl.BlockSpec(memory_space=pltpu.HBM)
SPACES = {id(VMEM): pltpu.VMEM, id(HBM): pltpu.HBM}


def in_hbm(values):
    return pltpu.with_memory_space_constraint(values, pltpu.HBM)


def run(body, name, ins, outs, scratch=(), out_specs=None, after=(), cost=0):
    count, total = len(ins), len(ins) + len(after)
    end = total + len(outs)

    def marked(*refs):
        body(*refs[:count], *refs[total:end], *refs[end + 1 :])
        refs[end][...] = jnp.zeros_like(refs[end])

    ins = list(ins) + [(VMEM, value) for value in after]
    args = [
        pltpu.with_memory_space_constraint(arg, SPACES[id(spec)]) if id(spec) in SPACES else arg
        for spec, arg in ins
    ]
    out_specs = list(out_specs or [VMEM] * len(outs)) + [VMEM]
    outs = list(outs) + [jax.ShapeDtypeStruct((8, 128), f32)]
    return pl.pallas_call(
        marked,
        name=name,
        out_shape=[
            SPACES[id(spec)](out.shape, out.dtype) if id(spec) in SPACES else out
            for spec, out in zip(out_specs, outs)
        ],
        in_specs=[spec for spec, _ in ins],
        out_specs=out_specs,
        scratch_shapes=list(scratch),
        cost_estimate=pl.CostEstimate(flops=cost, bytes_accessed=0, transcendentals=0),
        compiler_params=pltpu.CompilerParams(vmem_limit_bytes=VMEM_LIMIT),
    )(*args)


def split_local(
    groups, width, noise, buffer, reinit, slots, kernel_one, bias_one, kernel_two, bias_two, cotangent
):
    depth, pixels = noise.shape
    channels = kernel_one.shape[2]
    half = pixels // 2
    chips = width // 2
    block = 2 * depth
    rows = 9 * depth
    index = lax.axis_index("blk")
    core = index % 2
    chip = index // 2
    group = lax.axis_index("dp")
    shape = jax.ShapeDtypeStruct
    dma = pltpu.SemaphoreType.DMA

    first = [2, 4]

    def swap(values, axis, pairs, name):
        with jax.named_scope(name):
            return lax.ppermute(values, axis, pairs)

    def chip_swap(values, step, name):
        pairs = [(i, i ^ first[(step + i) % 2]) for i in range(width)]
        return swap(values, "blk", pairs, name)

    def core_swap(values, name):
        return swap(values, "blk", [(i, i ^ 1) for i in range(width)], name)

    line = {"in": [(0, 1), (3, 2)], "middle": [(1, 2), (2, 1)], "out": [(1, 0), (2, 3)]}

    def group_send(values, way, name):
        return swap(values, "dp", line[way], name + "_" + way)

    def order_of(which):
        swapped = jnp.where(which == 0, jnp.array([0, 1, 2, 3]), jnp.array([0, 2, 1, 3]))
        return jnp.bitwise_xor(chip, swapped).astype(jnp.int32)

    order, order_came = order_of(core), order_of(1 - core)
    core_at = core.reshape(1).astype(jnp.int32)
    inner = ((group == 1) | (group == 2)).reshape(1).astype(jnp.int32)

    def vmem(*values):
        return [(VMEM, value) for value in values]

    def like(*values):
        return [shape(value.shape, bf16) for value in values]

    own_one = kernel_one.reshape(rows, channels)
    own_two = kernel_two.reshape(rows, channels)
    other_two = core_swap(own_two, "kernel_two")
    other_one = core_swap(own_one, "kernel_one")
    bias_own = jnp.broadcast_to(bias_one[:, None], (depth, 128))
    bias_other = core_swap(bias_own, "bias")

    marks, phase = [], ["early"]

    def step(body, name, ins, outs, scratch=(), out_specs=None, also=()):
        after = marks[-1:] + list(also)
        costs = COSTS[phase[0]]
        cost = costs.get(name, costs["small" if name.split("_")[0] in SMALL else "big"])
        *results, mark = run(body, name, ins, outs, scratch, out_specs, after, cost)
        marks.append(mark)
        return results[0] if len(results) == 1 else results

    part = shape((depth, half), bf16)
    piece = shape((1, block, half), bf16)
    wide = shape((depth, pixels), bf16)
    field, keep, send = step(
        field_kernel,
        "field",
        [(SMEM, core_at)] + [(HBM, v) for v in (reinit, slots, noise, buffer, cotangent)],
        [wide, wide, wide],
        [
            pltpu.VMEM(noise.shape, bf16),
            pltpu.VMEM(buffer.shape, bf16),
            pltpu.VMEM(cotangent.shape, bf16),
            pltpu.VMEM(noise.shape, bf16),
            pltpu.SMEM(reinit.shape, jnp.int32),
            pltpu.SMEM(slots.shape, jnp.int32),
            dma((5,)),
        ],
    )
    came = core_swap(send, "pair")
    zero = step(place_kernel, "place", [(SMEM, core_at)] + vmem(keep, came), [piece])
    zero_near, zero_across = chip_swap(zero, 0, "zero_near"), chip_swap(zero, 1, "zero_across")

    def back(name, start, sends, *values):
        return step(
            functools.partial(back_kernel, start),
            name,
            [(SMEM, order)]
            + vmem(*values[:2])
            + [(HBM, in_hbm(values[2])), (VMEM, values[3])],
            [shape((count, block, half), bf16) for count in sends]
            + [shape((chips // 2, block, half), f32)],
            [
                pltpu.VMEM((rows, half), bf16),
                pltpu.VMEM((rows, half), bf16),
                pltpu.VMEM((channels, TILE), f32),
                pltpu.VMEM((rows, channels), bf16),
                dma,
            ],
        )

    send, last, keep_two = back("back_two", half, (1, 1), keep, came, own_two, other_two)
    last_two = chip_swap(last, 1, "two_last")
    zero, zero_near, send = step(
        join_kernel,
        "join_1",
        vmem(zero, zero_near, zero_across, send),
        [shape((3, block, half), bf16)] + like(zero_near, send),
        also=[other_one, bias_other],
    )
    zero_beyond = chip_swap(zero_near, 1, "zero_beyond")
    zero_came = core_swap(zero, "zero_pair")
    onward = step(onward_kernel, "onward_1", vmem(keep_two, last_two), [piece])
    far_two = chip_swap(onward, 0, "two_far")
    send, field = step(copy_kernel, "copy_1", vmem(send, field), like(send, field))
    near_two = chip_swap(send, 1, "two_near")
    zero_beyond = step(copy_kernel, "copy_2", vmem(zero_beyond), like(zero_beyond))
    beyond_came = core_swap(zero_beyond, "zero_pair_beyond")

    whole = shape((channels, half), bf16)
    plane = shape((depth, half), f32)
    whole_zero, pre_own, pre_other, one = step(
        conv_one_kernel,
        "conv_one",
        [(SMEM, core_at), (SMEM, order)]
        + vmem(zero, zero_beyond)
        + vmem(own_one, other_one, bias_own, bias_other),
        [whole, plane, plane, piece],
        [dma((chips,))],
    )

    pre_grad, pre_grad_send = step(
        slope_kernel,
        "slope",
        [(SMEM, core_at)] + vmem(keep_two, near_two, far_two, pre_own, pre_other),
        [part, part],
    )
    pre_grad_came = core_swap(pre_grad_send, "pre_grad")
    whole_zero_came = step(
        assemble_kernel,
        "assemble_1",
        [(SMEM, order_came)] + vmem(zero_came, beyond_came),
        [whole],
        [dma((chips,))],
    )

    def sizes(taps):
        return len(taps) * depth + (EXTRA if taps[-1] == 8 else 0)

    def grad_outs(taps):
        return [shape((sizes(taps), channels), bf16)]

    def grad_scratch(taps):
        return [
            pltpu.VMEM((sizes(taps), channels), f32),
            pltpu.VMEM((2, len(taps) * depth, half), bf16),
        ]

    def parts(ends):
        return [tuple(range(start, end)) for start, end in zip((0,) + ends[:-1], ends)]

    def add(name, left, right):
        return step(add_kernel, "add_" + name, vmem(left, right), like(left))

    phase[0] = "late"
    grads = []
    for at, taps in enumerate(parts(PARTS_ONE)):
        send = step(
            functools.partial(grad_one_kernel, taps),
            "grad_one_" + "ab"[at],
            vmem(pre_grad, pre_grad_came, whole_zero, whole_zero_came),
            grad_outs(taps),
            grad_scratch(taps),
        )
        grads.append(send)
        if at == 0:
            one = step(copy_kernel, "copy_3", vmem(one), like(one))
            one_near, one_across = chip_swap(one, 0, "one_near"), chip_swap(one, 1, "one_across")
    near_a = group_send(grads[0], "in", "one_a")
    send, keep_one = back("back_one", 0, (2,), pre_grad, pre_grad_send, own_one, other_one)
    send_one = send
    three, one_near = step(
        join_kernel,
        "join_one",
        vmem(one, one_near, one_across),
        [shape((3, block, half), bf16)] + like(one_near),
    )
    one_beyond = chip_swap(one_near, 1, "one_beyond")
    three_came = core_swap(three, "one_pair")

    send_b = step(copy_kernel, "copy_4", vmem(grads[1]), like(grads[1]))
    near_b = group_send(send_b, "in", "one_b")
    mine_a = add("one_a", grads[0], near_a)
    far_a = group_send(mine_a, "middle", "one_a")

    one_beyond = step(copy_kernel, "copy_beyond_one", vmem(one_beyond), like(one_beyond))
    beyond_came = core_swap(one_beyond, "one_pair_beyond")
    whole_one = step(
        assemble_kernel,
        "assemble_one",
        [(SMEM, order)] + vmem(three, one_beyond),
        [whole],
        [dma((chips,))],
    )
    whole_one_came = step(
        assemble_kernel,
        "assemble_one_came",
        [(SMEM, order_came)] + vmem(three_came, beyond_came),
        [whole],
        [dma((chips,))],
    )

    send_a, keep_b = step(
        grad_two_kernel,
        "grad_two",
        [(SMEM, core_at)] + vmem(cotangent, whole_one, whole_one_came),
        [out for taps in parts(PARTS_TWO) for out in grad_outs(taps)],
        grad_scratch(tuple(range(9))),
    )
    near_a = group_send(send_a, "in", "two_a")
    mine_b = add("one_b", send_b, near_b)
    far_b = group_send(mine_b, "middle", "one_b")
    send_b = step(copy_kernel, "copy_6", vmem(keep_b), like(keep_b))
    near_b = group_send(send_b, "in", "two_b")
    half_a = add("one_a_half", mine_a, far_a)
    rest_a = group_send(half_a, "out", "one_a")
    out_own, out_other = step(
        conv_two_kernel, "conv_two", vmem(whole_one, own_two, other_two), [plane, plane]
    )
    mine_two_a = add("two_a", send_a, near_a)
    far_two_a = group_send(mine_two_a, "middle", "two_a")
    half_b = add("one_b_half", mine_b, far_b)
    rest_b = group_send(half_b, "out", "one_b")
    mine_two_b = add("two_b", send_b, near_b)
    far_two_b = group_send(mine_two_b, "middle", "two_b")
    rest_a = step(copy_kernel, "copy_7", vmem(rest_a), like(rest_a))
    send_one = step(copy_kernel, "copy_5", vmem(send_one), like(send_one))
    near_one = chip_swap(send_one, 1, "one_near")
    half_two_a = add("two_a_half", mine_two_a, far_two_a)
    rest_two_a = group_send(half_two_a, "out", "two_a")

    def finish(name, pieces):
        kernel_grad, bias_grad = step(
            finish_kernel,
            name,
            [(SMEM, inner)] + vmem(*pieces),
            [shape((rows, channels), f32), shape((1, depth), f32)],
            [pltpu.VMEM((rows + EXTRA, channels), f32), dma((len(pieces) // 2,))],
            out_specs=[ANY, VMEM],
        )
        return kernel_grad.reshape(9, depth, channels), bias_grad.reshape(depth)

    kernel_grad_one, bias_grad_one = finish("finish_one", [half_a, rest_a, half_b, rest_b])
    half_two_b = add("two_b_half", mine_two_b, far_two_b)
    rest_two_b = group_send(half_two_b, "out", "two_b")
    onward = step(onward_kernel, "onward_2", vmem(keep_one, near_one), [piece])
    far_one = chip_swap(onward, 0, "one_far")
    out_other = step(copy_kernel, "copy_9", vmem(out_other), [plane])
    out_came = core_swap(out_other, "out_pair")
    own, other = step(
        sum_kernel, "sum", [(SMEM, core_at)] + vmem(keep_one, near_one, far_one), [plane, plane]
    )
    other = core_swap(other, "field_pair")
    rest_two_a = step(copy_kernel, "copy_10", vmem(rest_two_a), like(rest_two_a))
    output = step(
        output_kernel,
        "output",
        [(SMEM, core_at)]
        + vmem(field, out_own, out_came, jnp.broadcast_to(bias_two[:, None], (depth, 128))),
        [wide],
        [pltpu.VMEM((depth, pixels), bf16), dma],
        out_specs=[ANY],
    )
    grad_field = step(
        field_grad_kernel,
        "field_grad",
        [(SMEM, core_at)] + vmem(field, cotangent, own, other),
        [shape((depth, pixels), f32)],
        [pltpu.VMEM((depth, pixels), f32), dma],
        out_specs=[ANY],
    )
    kernel_grad_two, bias_grad_two = finish(
        "finish_two", [half_two_a, rest_two_a, half_two_b, rest_two_b]
    )
    return output, grad_field, kernel_grad_one, bias_grad_one, kernel_grad_two, bias_grad_two


def shift_tap(field, row, col):
    depth = field.shape[0]
    grid = field.reshape(depth, -1, 8, 8)
    grid = jnp.pad(grid, ((0, 0), (0, 0), (1, 1), (1, 1)))
    grid = grid[:, :, 1 + row : 9 + row, 1 + col : 9 + col]
    return grid.reshape(depth, -1)


def add_conv(total, piece, kernel):
    for number, (row, col) in enumerate(offsets):
        total = total + jnp.dot(
            kernel[number], shift_tap(piece, row, col), preferred_element_type=f32
        )
    return total


def add_grad(piece, upstream):
    parts = [
        lax.dot_general(
            upstream,
            shift_tap(piece, row, col),
            (((1,), (1,)), ((), ())),
            preferred_element_type=f32,
        )
        for row, col in offsets
    ]
    return jnp.stack(parts, 0)


def back_shifts(upstream):
    return jnp.stack([shift_tap(upstream, -row, -col) for row, col in offsets], 0)


def spread_rows(kernel, moved):
    return lax.dot_general(kernel, moved, (((0, 1), (0, 1)), ((), ())), preferred_element_type=f32)


def plain_local(
    noise, buffer, reinit, slots, kernel_one, bias_one, kernel_two, bias_two, cotangent
):
    depth = noise.shape[0]
    images = reinit.shape[0]
    pixels = images * 64
    stored = buffer.reshape(depth, -1, 64)[:, slots, :]
    fresh = noise.reshape(depth, images, 64)
    field = (
        jnp.where(reinit[None, :, None] == 1, fresh, stored).reshape(depth, pixels).astype(f32)
    )
    act_zero = jax.nn.silu(field).astype(bf16)
    empty = jnp.zeros((depth, pixels), f32)
    whole_zero = lax.all_gather(act_zero, "blk", axis=0, tiled=True)
    pre_one = add_conv(empty, whole_zero, kernel_one)
    pre_one = pre_one + bias_one.astype(f32)[:, None]
    act_one = jax.nn.silu(pre_one).astype(bf16)
    whole_one = lax.all_gather(act_one, "blk", axis=0, tiled=True)
    pre_two = add_conv(empty, whole_one, kernel_two)
    output = (field + pre_two + bias_two.astype(f32)[:, None]).astype(bf16)
    bias_grad_two = jnp.sum(cotangent.astype(f32), axis=1)
    kernel_grad_two = add_grad(whole_one, cotangent)
    grad_act_one = lax.psum_scatter(
        spread_rows(kernel_two, back_shifts(cotangent)), "blk", scatter_dimension=0, tiled=True
    )
    grad_pre_one = (grad_act_one * silu_slope(pre_one)).astype(bf16)
    bias_grad_one = jnp.sum(grad_pre_one.astype(f32), axis=1)
    kernel_grad_one = add_grad(whole_zero, grad_pre_one)
    grad_act_zero = lax.psum_scatter(
        spread_rows(kernel_one, back_shifts(grad_pre_one)).astype(bf16),
        "blk",
        scatter_dimension=0,
        tiled=True,
    ).astype(f32)
    grad_field = cotangent.astype(f32) + grad_act_zero * silu_slope(field)
    summed = lax.psum((kernel_grad_one, bias_grad_one, kernel_grad_two, bias_grad_two), "dp")
    return (output, grad_field, summed[0], summed[1], summed[2], summed[3])


def solution(mesh):
    groups, width = mesh.shape["dp"], mesh.shape["blk"]

    def local(noise, *rest):
        if groups == 4 and width == 8 and noise.shape[0] % 16 == 0 and noise.shape[1] % 512 == 0:
            return split_local(groups, width, noise, *rest)
        return plain_local(noise, *rest)

    return jax.shard_map(
        local,
        mesh=mesh,
        in_specs=(
            P("blk", "dp"),
            P("blk", "dp"),
            P("dp"),
            P("dp"),
            P(None, "blk", None),
            P("blk"),
            P(None, "blk", None),
            P("blk"),
            P("blk", "dp"),
        ),
        out_specs=(
            P("blk", "dp"),
            P("blk", "dp"),
            P(None, "blk", None),
            P("blk"),
            P(None, "blk", None),
            P("blk"),
        ),
        check_vma=False,
    )
```

```python
import functools

import jax
import jax.numpy as jnp
from jax import lax
from jax.experimental import pallas as pl
from jax.experimental.pallas import tpu as pltpu
from jax.sharding import PartitionSpec as P

bf16 = jnp.bfloat16
f32 = jnp.float32
offsets = [(row, col) for row in (-1, 0, 1) for col in (-1, 0, 1)]
VMEM_LIMIT = 20 << 20
COSTS = {'early': {'big': 10000000000, 'small': 0, 'slope': 0}, 'late': {'big': 20000000000, 'small': 500000000, 'assemble_one': 30000000000, 'copy': 0, 'add_one_a': 100000000, 'assemble_one_came': 500000000, 'add_one_b': 10000000000, 'copy_6': 1000000000, 'add_one_a_half': 1000000000, 'add_one_b_half': 500000000, 'copy_7': 3000000000, 'back_one': 30000000000, 'conv_two': 100000000, 'grad_one_b': 1000000000, 'copy_beyond_one': 100000000, 'output': 100000000000, 'copy_10': 30000000000, 'field_grad': 10000000000, 'finish_two': 100000000000, 'sum': 1000000000, 'join_one': 30000000000, 'finish_one': 10000000000, 'add_two_a': 1000000000, 'add_two_b_half': 100000000, 'onward_2': 0, 'grad_one_a': 500000000}}
SMALL = ("place", "copy", "add", "join", "onward", "sum", "assemble")
EXTRA = 16
PARTS_ONE, PARTS_TWO = (5, 9), (5, 9)
TILE = 256
CONV_TILE = 512


def silu_slope(value):
    sigma = jax.nn.sigmoid(value)
    return sigma * (1.0 + value * (1.0 - sigma))


def inside(width, row, col):
    pixel = lax.broadcasted_iota(jnp.int32, (1, width), 1)
    r = ((pixel >> 3) & 7) + row
    s = (pixel & 7) + col
    return (r >= 0) & (r < 8) & (s >= 0) & (s < 8)


def shifted(values, row, col):
    step = 8 * row + col
    if step == 0:
        return values
    kept = inside(128, row, col)
    pieces = []
    for start in range(0, values.shape[1], 128):
        moved = pltpu.roll(values[:, start : start + 128], (-step) % 128, 1)
        pieces.append(jnp.where(kept, moved, jnp.zeros_like(moved)))
    return jnp.concatenate(pieces, 1) if len(pieces) > 1 else pieces[0]


def field_kernel(
    core, reinit, slots, noise, buffer, cotangent, field, keep, send, fresh, stored, cot, act, fresh_at, slot_at, sem
):
    pixels = field.shape[1]
    half = pixels // 2
    lane = lax.broadcasted_iota(jnp.int32, (1, 128), 1)
    sources = (reinit, slots, noise, buffer, cotangent)
    places = (fresh_at, slot_at, fresh, stored, cot)
    copies = [
        pltpu.make_async_copy(source, place, sem.at[at])
        for at, (source, place) in enumerate(zip(sources, places))
    ]
    for copy in copies:
        copy.start()
    for copy in copies:
        copy.wait()

    def place(image, block):
        slot = slot_at[image]
        found = stored[:, pl.ds(pl.multiple_of((slot >> 1) * 128, 128), 128)]
        found = jnp.where((slot & 1) == (image & 1), found, pltpu.roll(found, 64, 1))
        return jnp.where(fresh_at[image] == 1, block, found)

    for pair in range(pixels // 128):
        here = pl.ds(pair * 128, 128)
        block = fresh[:, here]
        value = jnp.where(lane < 64, place(2 * pair, block), place(2 * pair + 1, block))
        field[:, here] = value
        value = value.astype(f32)
        act[:, here] = (value * jax.nn.sigmoid(value)).astype(bf16)

    for at, out in ((core[0], keep), (1 - core[0], send)):
        lanes = pl.ds(pl.multiple_of(at * half, 128), half)
        out[:, :half] = act[:, lanes]
        out[:, half:] = cot[:, lanes]


def place_kernel(core, keep, came, block):
    depth, half = keep.shape[0], block.shape[2]
    for at, part in ((core[0], keep), (1 - core[0], came)):
        block[0, pl.ds(pl.multiple_of(at * depth, 16), depth), :] = part[:, :half]


def write_shifts(stack, values, taps=range(9)):
    depth = values.shape[0]
    for at, tap in enumerate(taps):
        row, col = offsets[tap]
        stack[pl.ds(at * depth, depth), :] = shifted(values, -row, -col)


def back_kernel(start, order, own, other, kernel_own, kernel_other, *refs):
    *sends, keep, stack_own, stack_other, block, held, sem = refs
    copy = pltpu.make_async_copy(kernel_own, held, sem)
    copy.start()
    half, depth, pixels = keep.shape
    places = [send.at[at] for send in sends for at in range(send.shape[0])]
    write_shifts(stack_own, own[:, start : start + pixels])
    write_shifts(stack_other, other[:, start : start + pixels])
    copy.wait()

    def step(at, _):
        lanes = pl.ds(pl.multiple_of(at * TILE, TILE), TILE)
        total = None
        for kernel, stack in ((held, stack_own), (kernel_other, stack_other)):
            part = lax.dot_general(
                kernel[...], stack[:, lanes], (((0,), (0,)), ((), ())), preferred_element_type=f32
            )
            total = part if total is None else total + part
        block[...] = total
        for slot in range(2 * half):
            rows = block[pl.ds(pl.multiple_of(order[slot] * depth, 8), depth), :]
            if slot < half:
                keep[slot, :, lanes] = rows
            else:
                places[slot - half][:, lanes] = rows.astype(bf16)
        return 0

    lax.fori_loop(0, pixels // TILE, step, 0)


def fetch(order, pieces, whole, sem):
    copies = []
    for piece in pieces:
        for at in range(piece.shape[0]):
            slot, depth = len(copies), piece.shape[1]
            start = pl.multiple_of(order[slot] * depth, 16)
            copies.append(
                pltpu.make_async_copy(piece.at[at], whole.at[pl.ds(start, depth), :], sem.at[slot])
            )
            copies[-1].start()
    return copies


def conv_tile(kernel, tile):
    depth = kernel.shape[0] // 9
    spread = jnp.dot(kernel[...], tile, preferred_element_type=f32)
    total = spread[4 * depth : 5 * depth]
    for tap, (row, col) in enumerate(offsets):
        if tap != 4:
            total = total + shifted(spread[tap * depth : (tap + 1) * depth], row, col)
    return total


def conv_one_kernel(
    core, order, three, beyond, kernel_own, kernel_other, bias_own, bias_other, whole, pre_own, pre_other, act, sem
):
    for copy in fetch(order, (three, beyond), whole, sem):
        copy.wait()
    depth = pre_own.shape[0]

    def step(at, _):
        lanes = pl.ds(pl.multiple_of(at * CONV_TILE, CONV_TILE), CONV_TILE)
        tile = whole[:, lanes]
        for kernel, bias, pre, place in (
            (kernel_own, bias_own, pre_own, core[0]),
            (kernel_other, bias_other, pre_other, 1 - core[0]),
        ):
            value = conv_tile(kernel, tile) + bias[:, :1].astype(f32)
            pre[:, lanes] = value
            rows = pl.ds(pl.multiple_of(place * depth, 16), depth)
            act[0, rows, lanes] = (value * jax.nn.sigmoid(value)).astype(bf16)
        return 0

    lax.fori_loop(0, whole.shape[1] // CONV_TILE, step, 0)


def conv_two_kernel(whole, kernel_own, kernel_other, out_own, out_other):
    def step(at, _):
        lanes = pl.ds(pl.multiple_of(at * CONV_TILE, CONV_TILE), CONV_TILE)
        tile = whole[:, lanes]
        out_own[:, lanes] = conv_tile(kernel_own, tile)
        out_other[:, lanes] = conv_tile(kernel_other, tile)
        return 0

    lax.fori_loop(0, whole.shape[1] // CONV_TILE, step, 0)


def slope_kernel(core, kept, near, far, pre_own, pre_other, own, other):
    depth = own.shape[0]
    for pre, place, out in ((pre_own, core[0], own), (pre_other, 1 - core[0], other)):
        rows = pl.ds(pl.multiple_of(place * depth, 16), depth)
        upstream = kept[0, rows, :] + near[0, rows, :].astype(f32) + far[0, rows, :].astype(f32)
        out[...] = (upstream * silu_slope(pre[...])).astype(bf16)


def write_grad(taps, parts, outs, grad, stacks):
    transposed = (((1,), (1,)), ((), ()))
    depth = parts[0][0].shape[0]
    rows = len(taps) * depth
    total = sums = None
    for at, (values, whole) in enumerate(parts):
        write_shifts(stacks.at[at], values, taps)
        part = lax.dot_general(stacks[at], whole[...], transposed, preferred_element_type=f32)
        total = part if total is None else total + part
        if taps[-1] == 8:
            ones = jnp.ones((EXTRA, values.shape[1]), bf16)
            part = lax.dot_general(ones, values, transposed, preferred_element_type=f32)
            sums = part if sums is None else sums + part
    grad[:rows, :] = total
    if taps[-1] == 8:
        grad[rows:, :] = jnp.zeros((EXTRA, grad.shape[1]), f32)
        grad[rows:, :depth] = sums
    base = 0
    for out in outs:
        size = out.shape[0]
        out[...] = grad[base : base + size, :].astype(bf16)
        base += size


def grad_one_kernel(taps, own, came, whole, whole_came, out, grad, stacks):
    parts = (own[...], whole), (came[...], whole_came)
    write_grad(taps, parts, (out,), grad, stacks)


def grad_two_kernel(core, cotangent, whole, whole_came, *refs):
    *outs, grad, stacks = refs
    half = whole.shape[1]
    own, came = (
        cotangent[:, pl.ds(pl.multiple_of(at * half, 128), half)] for at in (core[0], 1 - core[0])
    )
    parts = (own, whole), (came, whole_came)
    write_grad(tuple(range(9)), parts, outs, grad, stacks)


def copy_kernel(*refs):
    for values, out in zip(refs[: len(refs) // 2], refs[len(refs) // 2 :]):
        out[...] = values[...]


def add_kernel(left, right, out):
    out[...] = (left[...].astype(f32) + right[...].astype(f32)).astype(bf16)


def join_kernel(own, near, across, *refs):
    others, (joined, *outs) = refs[: len(refs) // 2 - 1], refs[len(refs) // 2 - 1 :]
    for at, block in enumerate((own, near, across)):
        joined[at] = block[0]
    for values, out in zip((near, *others), outs):
        out[...] = values[...]


def assemble_kernel(order, *refs):
    *pieces, whole, sem = refs
    for copy in fetch(order, pieces, whole, sem):
        copy.wait()


def sum_kernel(core, kept, near, far, own, other):
    depth = own.shape[0]
    for place, out in ((core[0], own), (1 - core[0], other)):
        rows = pl.ds(pl.multiple_of(place * depth, 16), depth)
        out[...] = kept[0, rows, :] + near[0, rows, :].astype(f32) + far[0, rows, :].astype(f32)


def output_kernel(core, field, own, came, bias, out, total, sem):
    half = own.shape[1]
    column = bias[:, :1].astype(f32)
    for at, part in ((core[0], own), (1 - core[0], came)):
        lanes = pl.ds(pl.multiple_of(at * half, 128), half)
        total[:, lanes] = (field[:, lanes].astype(f32) + part[...] + column).astype(bf16)
    copy = pltpu.make_async_copy(total, out, sem)
    copy.start()
    copy.wait()


def field_grad_kernel(core, field, cotangent, own, came, out, total, sem):
    half = own.shape[1]
    for at, part in ((core[0], own), (1 - core[0], came)):
        lanes = pl.ds(pl.multiple_of(at * half, 128), half)
        slope = silu_slope(field[:, lanes].astype(f32))
        total[:, lanes] = cotangent[:, lanes].astype(f32) + part[...] * slope
    copy = pltpu.make_async_copy(total, out, sem)
    copy.start()
    copy.wait()


def onward_kernel(keep, near, out):
    out[0] = (keep[1] + near[near.shape[0] - 1].astype(f32)).astype(bf16)


def finish_kernel(inner, *refs):
    pieces, (grad, bias, total, sem) = refs[:-4], refs[-4:]
    base, copies, rows = 0, [], grad.shape[0]
    for at, (made, came) in enumerate(zip(pieces[0::2], pieces[1::2])):
        size = made.shape[0]
        value = jnp.where(inner[0] == 1, made[...], came[...])
        total[base : base + size, :] = value.astype(f32)
        span = pl.ds(base, min(size, rows - base))
        copies.append(pltpu.make_async_copy(total.at[span, :], grad.at[span, :], sem.at[at]))
        copies[-1].start()
        base += size
    bias[...] = total[rows, : bias.shape[0]]
    for copy in copies:
        copy.wait()


def finish_first_kernel(inner, made, came, grad, total, sem):
    total[...] = jnp.where(inner[0] == 1, made[...], came[...]).astype(f32)
    copy = pltpu.make_async_copy(total, grad.at[pl.ds(0, total.shape[0]), :], sem)
    copy.start()
    copy.wait()


def finish_last_kernel(inner, made, came, begun, grad, bias, total, sem):
    total[...] = jnp.where(inner[0] == 1, made[...], came[...]).astype(f32)
    count = total.shape[0] - EXTRA
    rows = pl.ds(grad.shape[0] - count, count)
    copy = pltpu.make_async_copy(total.at[pl.ds(0, count), :], grad.at[rows, :], sem)
    copy.start()
    bias[...] = total[count, : bias.shape[0]]
    copy.wait()


SMEM = pl.BlockSpec(memory_space=pltpu.SMEM)
VMEM = pl.BlockSpec(memory_space=pltpu.VMEM)
ANY = pl.BlockSpec(memory_space=pl.ANY)
HBM = pl.BlockSpec(memory_space=pltpu.HBM)
SPACES = {id(VMEM): pltpu.VMEM, id(HBM): pltpu.HBM}


def in_hbm(values):
    return pltpu.with_memory_space_constraint(values, pltpu.HBM)


def run(body, name, ins, outs, scratch=(), out_specs=None, after=(), cost=0, aliases=None):
    count, total = len(ins), len(ins) + len(after)
    end = total + len(outs)

    def marked(*refs):
        body(*refs[:count], *refs[total:end], *refs[end + 1 :])
        refs[end][...] = jnp.zeros_like(refs[end])

    ins = list(ins) + [(VMEM, value) for value in after]
    args = [
        pltpu.with_memory_space_constraint(arg, SPACES[id(spec)]) if id(spec) in SPACES else arg
        for spec, arg in ins
    ]
    out_specs = list(out_specs or [VMEM] * len(outs)) + [VMEM]
    outs = list(outs) + [jax.ShapeDtypeStruct((8, 128), f32)]
    return pl.pallas_call(
        marked,
        name=name,
        out_shape=[
            SPACES[id(spec)](out.shape, out.dtype) if id(spec) in SPACES else out
            for spec, out in zip(out_specs, outs)
        ],
        in_specs=[spec for spec, _ in ins],
        out_specs=out_specs,
        scratch_shapes=list(scratch),
        input_output_aliases=aliases or {},
        cost_estimate=pl.CostEstimate(flops=cost, bytes_accessed=0, transcendentals=0),
        compiler_params=pltpu.CompilerParams(vmem_limit_bytes=VMEM_LIMIT),
    )(*args)


def split_local(
    groups, width, noise, buffer, reinit, slots, kernel_one, bias_one, kernel_two, bias_two, cotangent
):
    depth, pixels = noise.shape
    channels = kernel_one.shape[2]
    half = pixels // 2
    chips = width // 2
    block = 2 * depth
    rows = 9 * depth
    index = lax.axis_index("blk")
    core = index % 2
    chip = index // 2
    group = lax.axis_index("dp")
    shape = jax.ShapeDtypeStruct
    dma = pltpu.SemaphoreType.DMA

    first = [2, 4]

    def swap(values, axis, pairs, name):
        with jax.named_scope(name):
            return lax.ppermute(values, axis, pairs)

    def chip_swap(values, step, name):
        pairs = [(i, i ^ first[(step + i) % 2]) for i in range(width)]
        return swap(values, "blk", pairs, name)

    def core_swap(values, name):
        return swap(values, "blk", [(i, i ^ 1) for i in range(width)], name)

    line = {"in": [(0, 1), (3, 2)], "middle": [(1, 2), (2, 1)], "out": [(1, 0), (2, 3)]}

    def group_send(values, way, name):
        return swap(values, "dp", line[way], name + "_" + way)

    def order_of(which):
        swapped = jnp.where(which == 0, jnp.array([0, 1, 2, 3]), jnp.array([0, 2, 1, 3]))
        return jnp.bitwise_xor(chip, swapped).astype(jnp.int32)

    order, order_came = order_of(core), order_of(1 - core)
    core_at = core.reshape(1).astype(jnp.int32)
    inner = ((group == 1) | (group == 2)).reshape(1).astype(jnp.int32)

    def vmem(*values):
        return [(VMEM, value) for value in values]

    def like(*values):
        return [shape(value.shape, bf16) for value in values]

    own_one = kernel_one.reshape(rows, channels)
    own_two = kernel_two.reshape(rows, channels)
    other_two = core_swap(own_two, "kernel_two")
    other_one = core_swap(own_one, "kernel_one")
    bias_own = jnp.broadcast_to(bias_one[:, None], (depth, 128))
    bias_other = core_swap(bias_own, "bias")

    marks, phase = [], ["early"]

    def step(body, name, ins, outs, scratch=(), out_specs=None, also=(), aliases=None):
        after = marks[-1:] + list(also)
        costs = COSTS[phase[0]]
        cost = costs.get(name, costs["small" if name.split("_")[0] in SMALL else "big"])
        *results, mark = run(body, name, ins, outs, scratch, out_specs, after, cost, aliases)
        marks.append(mark)
        return results[0] if len(results) == 1 else results

    part = shape((depth, half), bf16)
    piece = shape((1, block, half), bf16)
    wide = shape((depth, pixels), bf16)
    field, keep, send = step(
        field_kernel,
        "field",
        [(SMEM, core_at)] + [(HBM, v) for v in (reinit, slots, noise, buffer, cotangent)],
        [wide, wide, wide],
        [
            pltpu.VMEM(noise.shape, bf16),
            pltpu.VMEM(buffer.shape, bf16),
            pltpu.VMEM(cotangent.shape, bf16),
            pltpu.VMEM(noise.shape, bf16),
            pltpu.SMEM(reinit.shape, jnp.int32),
            pltpu.SMEM(slots.shape, jnp.int32),
            dma((5,)),
        ],
    )
    came = core_swap(send, "pair")
    zero = step(place_kernel, "place", [(SMEM, core_at)] + vmem(keep, came), [piece])
    zero_near, zero_across = chip_swap(zero, 0, "zero_near"), chip_swap(zero, 1, "zero_across")

    def back(name, start, sends, *values):
        return step(
            functools.partial(back_kernel, start),
            name,
            [(SMEM, order)]
            + vmem(*values[:2])
            + [(HBM, in_hbm(values[2])), (VMEM, values[3])],
            [shape((count, block, half), bf16) for count in sends]
            + [shape((chips // 2, block, half), f32)],
            [
                pltpu.VMEM((rows, half), bf16),
                pltpu.VMEM((rows, half), bf16),
                pltpu.VMEM((channels, TILE), f32),
                pltpu.VMEM((rows, channels), bf16),
                dma,
            ],
        )

    send, last, keep_two = back("back_two", half, (1, 1), keep, came, own_two, other_two)
    last_two = chip_swap(last, 1, "two_last")
    zero, zero_near, send = step(
        join_kernel,
        "join_1",
        vmem(zero, zero_near, zero_across, send),
        [shape((3, block, half), bf16)] + like(zero_near, send),
        also=[other_one, bias_other],
    )
    zero_beyond = chip_swap(zero_near, 1, "zero_beyond")
    zero_came = core_swap(zero, "zero_pair")
    onward = step(onward_kernel, "onward_1", vmem(keep_two, last_two), [piece])
    far_two = chip_swap(onward, 0, "two_far")
    send, field = step(copy_kernel, "copy_1", vmem(send, field), like(send, field))
    near_two = chip_swap(send, 1, "two_near")
    zero_beyond = step(copy_kernel, "copy_2", vmem(zero_beyond), like(zero_beyond))
    beyond_came = core_swap(zero_beyond, "zero_pair_beyond")

    whole = shape((channels, half), bf16)
    plane = shape((depth, half), f32)
    whole_zero, pre_own, pre_other, one = step(
        conv_one_kernel,
        "conv_one",
        [(SMEM, core_at), (SMEM, order)]
        + vmem(zero, zero_beyond)
        + vmem(own_one, other_one, bias_own, bias_other),
        [whole, plane, plane, piece],
        [dma((chips,))],
    )

    pre_grad, pre_grad_send = step(
        slope_kernel,
        "slope",
        [(SMEM, core_at)] + vmem(keep_two, near_two, far_two, pre_own, pre_other),
        [part, part],
    )
    pre_grad_came = core_swap(pre_grad_send, "pre_grad")
    whole_zero_came = step(
        assemble_kernel,
        "assemble_1",
        [(SMEM, order_came)] + vmem(zero_came, beyond_came),
        [whole],
        [dma((chips,))],
    )

    def sizes(taps):
        return len(taps) * depth + (EXTRA if taps[-1] == 8 else 0)

    def grad_outs(taps):
        return [shape((sizes(taps), channels), bf16)]

    def grad_scratch(taps):
        return [
            pltpu.VMEM((sizes(taps), channels), f32),
            pltpu.VMEM((2, len(taps) * depth, half), bf16),
        ]

    def parts(ends):
        return [tuple(range(start, end)) for start, end in zip((0,) + ends[:-1], ends)]

    def add(name, left, right):
        return step(add_kernel, "add_" + name, vmem(left, right), like(left))

    phase[0] = "late"
    grads = []
    for at, taps in enumerate(parts(PARTS_ONE)):
        send = step(
            functools.partial(grad_one_kernel, taps),
            "grad_one_" + "ab"[at],
            vmem(pre_grad, pre_grad_came, whole_zero, whole_zero_came),
            grad_outs(taps),
            grad_scratch(taps),
        )
        grads.append(send)
        if at == 0:
            one = step(copy_kernel, "copy_3", vmem(one), like(one))
            one_near, one_across = chip_swap(one, 0, "one_near"), chip_swap(one, 1, "one_across")
    near_a = group_send(grads[0], "in", "one_a")
    send, keep_one = back("back_one", 0, (2,), pre_grad, pre_grad_send, own_one, other_one)
    send_one = send
    three, one_near = step(
        join_kernel,
        "join_one",
        vmem(one, one_near, one_across),
        [shape((3, block, half), bf16)] + like(one_near),
    )
    one_beyond = chip_swap(one_near, 1, "one_beyond")
    three_came = core_swap(three, "one_pair")

    send_b = step(copy_kernel, "copy_4", vmem(grads[1]), like(grads[1]))
    near_b = group_send(send_b, "in", "one_b")
    mine_a = add("one_a", grads[0], near_a)
    far_a = group_send(mine_a, "middle", "one_a")

    one_beyond = step(copy_kernel, "copy_beyond_one", vmem(one_beyond), like(one_beyond))
    beyond_came = core_swap(one_beyond, "one_pair_beyond")
    whole_one = step(
        assemble_kernel,
        "assemble_one",
        [(SMEM, order)] + vmem(three, one_beyond),
        [whole],
        [dma((chips,))],
    )
    whole_one_came = step(
        assemble_kernel,
        "assemble_one_came",
        [(SMEM, order_came)] + vmem(three_came, beyond_came),
        [whole],
        [dma((chips,))],
    )

    send_a, keep_b = step(
        grad_two_kernel,
        "grad_two",
        [(SMEM, core_at)] + vmem(cotangent, whole_one, whole_one_came),
        [out for taps in parts(PARTS_TWO) for out in grad_outs(taps)],
        grad_scratch(tuple(range(9))),
    )
    near_a = group_send(send_a, "in", "two_a")
    mine_b = add("one_b", send_b, near_b)
    far_b = group_send(mine_b, "middle", "one_b")
    send_b = step(copy_kernel, "copy_6", vmem(keep_b), like(keep_b))
    near_b = group_send(send_b, "in", "two_b")
    half_a = add("one_a_half", mine_a, far_a)
    rest_a = group_send(half_a, "out", "one_a")
    out_own, out_other = step(
        conv_two_kernel, "conv_two", vmem(whole_one, own_two, other_two), [plane, plane]
    )
    mine_two_a = add("two_a", send_a, near_a)
    far_two_a = group_send(mine_two_a, "middle", "two_a")
    half_b = add("one_b_half", mine_b, far_b)
    rest_b = group_send(half_b, "out", "one_b")
    mine_two_b = add("two_b", send_b, near_b)
    far_two_b = group_send(mine_two_b, "middle", "two_b")
    rest_a = step(copy_kernel, "copy_7", vmem(rest_a), like(rest_a))
    send_one = step(copy_kernel, "copy_5", vmem(send_one), like(send_one))
    near_one = chip_swap(send_one, 1, "one_near")
    half_two_a = add("two_a_half", mine_two_a, far_two_a)
    rest_two_a = group_send(half_two_a, "out", "two_a")

    def finish(name, pieces):
        kernel_grad, bias_grad = step(
            finish_kernel,
            name,
            [(SMEM, inner)] + vmem(*pieces),
            [shape((rows, channels), f32), shape((depth,), f32)],
            [pltpu.VMEM((rows + EXTRA, channels), f32), dma((len(pieces) // 2,))],
            out_specs=[ANY, VMEM],
        )
        return kernel_grad.reshape(9, depth, channels), bias_grad

    kernel_grad_one, bias_grad_one = finish("finish_one", [half_a, rest_a, half_b, rest_b])
    half_two_b = add("two_b_half", mine_two_b, far_two_b)
    rest_two_b = group_send(half_two_b, "out", "two_b")
    onward = step(onward_kernel, "onward_2", vmem(keep_one, near_one), [piece])
    far_one = chip_swap(onward, 0, "one_far")
    out_other = step(copy_kernel, "copy_9", vmem(out_other), [plane])
    out_came = core_swap(out_other, "out_pair")
    own, other = step(
        sum_kernel, "sum", [(SMEM, core_at)] + vmem(keep_one, near_one, far_one), [plane, plane]
    )
    other = core_swap(other, "field_pair")
    begun = step(
        finish_first_kernel,
        "finish_two_first",
        [(SMEM, inner)] + vmem(half_two_a, rest_two_a),
        [shape((rows, channels), f32)],
        [pltpu.VMEM(half_two_a.shape, f32), dma],
        out_specs=[ANY],
    )
    output = step(
        output_kernel,
        "output",
        [(SMEM, core_at)]
        + vmem(field, out_own, out_came, jnp.broadcast_to(bias_two[:, None], (depth, 128))),
        [wide],
        [pltpu.VMEM((depth, pixels), bf16), dma],
        out_specs=[ANY],
    )
    grad_field = step(
        field_grad_kernel,
        "field_grad",
        [(SMEM, core_at)] + vmem(field, cotangent, own, other),
        [shape((depth, pixels), f32)],
        [pltpu.VMEM((depth, pixels), f32), dma],
        out_specs=[ANY],
    )
    count = half_two_b.shape[0]
    kernel_grad_two, bias_grad_two = step(
        finish_last_kernel,
        "finish_two",
        [(SMEM, inner)] + vmem(half_two_b, rest_two_b) + [(ANY, begun)],
        [shape((rows, channels), f32), shape((depth,), f32)],
        [pltpu.VMEM((count, channels), f32), dma],
        out_specs=[ANY, VMEM],
        aliases={3: 0},
    )
    kernel_grad_two = kernel_grad_two.reshape(9, depth, channels)
    return output, grad_field, kernel_grad_one, bias_grad_one, kernel_grad_two, bias_grad_two


def shift_tap(field, row, col):
    depth = field.shape[0]
    grid = field.reshape(depth, -1, 8, 8)
    grid = jnp.pad(grid, ((0, 0), (0, 0), (1, 1), (1, 1)))
    grid = grid[:, :, 1 + row : 9 + row, 1 + col : 9 + col]
    return grid.reshape(depth, -1)


def add_conv(total, piece, kernel):
    for number, (row, col) in enumerate(offsets):
        total = total + jnp.dot(
            kernel[number], shift_tap(piece, row, col), preferred_element_type=f32
        )
    return total


def add_grad(piece, upstream):
    parts = [
        lax.dot_general(
            upstream,
            shift_tap(piece, row, col),
            (((1,), (1,)), ((), ())),
            preferred_element_type=f32,
        )
        for row, col in offsets
    ]
    return jnp.stack(parts, 0)


def back_shifts(upstream):
    return jnp.stack([shift_tap(upstream, -row, -col) for row, col in offsets], 0)


def spread_rows(kernel, moved):
    return lax.dot_general(kernel, moved, (((0, 1), (0, 1)), ((), ())), preferred_element_type=f32)


def plain_local(
    noise, buffer, reinit, slots, kernel_one, bias_one, kernel_two, bias_two, cotangent
):
    depth = noise.shape[0]
    images = reinit.shape[0]
    pixels = images * 64
    stored = buffer.reshape(depth, -1, 64)[:, slots, :]
    fresh = noise.reshape(depth, images, 64)
    field = (
        jnp.where(reinit[None, :, None] == 1, fresh, stored).reshape(depth, pixels).astype(f32)
    )
    act_zero = jax.nn.silu(field).astype(bf16)
    empty = jnp.zeros((depth, pixels), f32)
    whole_zero = lax.all_gather(act_zero, "blk", axis=0, tiled=True)
    pre_one = add_conv(empty, whole_zero, kernel_one)
    pre_one = pre_one + bias_one.astype(f32)[:, None]
    act_one = jax.nn.silu(pre_one).astype(bf16)
    whole_one = lax.all_gather(act_one, "blk", axis=0, tiled=True)
    pre_two = add_conv(empty, whole_one, kernel_two)
    output = (field + pre_two + bias_two.astype(f32)[:, None]).astype(bf16)
    bias_grad_two = jnp.sum(cotangent.astype(f32), axis=1)
    kernel_grad_two = add_grad(whole_one, cotangent)
    grad_act_one = lax.psum_scatter(
        spread_rows(kernel_two, back_shifts(cotangent)), "blk", scatter_dimension=0, tiled=True
    )
    grad_pre_one = (grad_act_one * silu_slope(pre_one)).astype(bf16)
    bias_grad_one = jnp.sum(grad_pre_one.astype(f32), axis=1)
    kernel_grad_one = add_grad(whole_zero, grad_pre_one)
    grad_act_zero = lax.psum_scatter(
        spread_rows(kernel_one, back_shifts(grad_pre_one)).astype(bf16),
        "blk",
        scatter_dimension=0,
        tiled=True,
    ).astype(f32)
    grad_field = cotangent.astype(f32) + grad_act_zero * silu_slope(field)
    summed = lax.psum((kernel_grad_one, bias_grad_one, kernel_grad_two, bias_grad_two), "dp")
    return (output, grad_field, summed[0], summed[1], summed[2], summed[3])


def solution(mesh):
    groups, width = mesh.shape["dp"], mesh.shape["blk"]

    def local(noise, *rest):
        if groups == 4 and width == 8 and noise.shape[0] % 16 == 0 and noise.shape[1] % 512 == 0:
            return split_local(groups, width, noise, *rest)
        return plain_local(noise, *rest)

    return jax.shard_map(
        local,
        mesh=mesh,
        in_specs=(
            P("blk", "dp"),
            P("blk", "dp"),
            P("dp"),
            P("dp"),
            P(None, "blk", None),
            P("blk"),
            P(None, "blk", None),
            P("blk"),
            P("blk", "dp"),
        ),
        out_specs=(
            P("blk", "dp"),
            P("blk", "dp"),
            P(None, "blk", None),
            P("blk"),
            P(None, "blk", None),
            P("blk"),
        ),
        check_vma=False,
    )
```

```python
import functools

import jax
import jax.numpy as jnp
from jax import lax
from jax.experimental import pallas as pl
from jax.experimental.pallas import tpu as pltpu
from jax.sharding import PartitionSpec as P

bf16 = jnp.bfloat16
f32 = jnp.float32
offsets = [(row, col) for row in (-1, 0, 1) for col in (-1, 0, 1)]
VMEM_LIMIT = 20 << 20
COSTS = {'early': {'big': 10000000000, 'small': 0, 'slope': 0}, 'late': {'big': 20000000000, 'small': 500000000, 'assemble_one': 30000000000, 'copy': 0, 'add_one_a': 100000000, 'assemble_one_came': 500000000, 'add_one_b': 10000000000, 'copy_6': 1000000000, 'add_one_a_half': 1000000000, 'add_one_b_half': 500000000, 'copy_7': 3000000000, 'back_one': 30000000000, 'conv_two': 100000000, 'grad_one_b': 1000000000, 'copy_beyond_one': 100000000, 'output': 100000000000, 'copy_10': 30000000000, 'field_grad': 10000000000, 'finish_two': 100000000000, 'sum': 1000000000, 'join_one': 30000000000, 'finish_one': 10000000000, 'add_two_a': 1000000000, 'add_two_b_half': 100000000, 'onward_2': 0, 'grad_one_a': 500000000}}
SMALL = ("place", "copy", "add", "join", "onward", "sum", "assemble")
EXTRA = 16
PARTS_ONE, PARTS_TWO = (5, 9), (5, 9)
TILE = 512
CONV_TILE = 512


def silu_slope(value):
    sigma = jax.nn.sigmoid(value)
    return sigma * (1.0 + value * (1.0 - sigma))


def inside(width, row, col):
    pixel = lax.broadcasted_iota(jnp.int32, (1, width), 1)
    r = ((pixel >> 3) & 7) + row
    s = (pixel & 7) + col
    return (r >= 0) & (r < 8) & (s >= 0) & (s < 8)


def shifted(values, row, col):
    step = 8 * row + col
    if step == 0:
        return values
    kept = inside(128, row, col)
    pieces = []
    for start in range(0, values.shape[1], 128):
        moved = pltpu.roll(values[:, start : start + 128], (-step) % 128, 1)
        pieces.append(jnp.where(kept, moved, jnp.zeros_like(moved)))
    return jnp.concatenate(pieces, 1) if len(pieces) > 1 else pieces[0]


def field_kernel(
    core, reinit, slots, noise, buffer, cotangent, field, keep, send, fresh, stored, cot, act, fresh_at, slot_at, sem
):
    pixels = field.shape[1]
    half = pixels // 2
    lane = lax.broadcasted_iota(jnp.int32, (1, 128), 1)
    sources = (reinit, slots, noise, buffer, cotangent)
    places = (fresh_at, slot_at, fresh, stored, cot)
    copies = [
        pltpu.make_async_copy(source, place, sem.at[at])
        for at, (source, place) in enumerate(zip(sources, places))
    ]
    for copy in copies:
        copy.start()
    for copy in copies:
        copy.wait()

    def place(image, block):
        slot = slot_at[image]
        found = stored[:, pl.ds(pl.multiple_of((slot >> 1) * 128, 128), 128)]
        found = jnp.where((slot & 1) == (image & 1), found, pltpu.roll(found, 64, 1))
        return jnp.where(fresh_at[image] == 1, block, found)

    for pair in range(pixels // 128):
        here = pl.ds(pair * 128, 128)
        block = fresh[:, here]
        value = jnp.where(lane < 64, place(2 * pair, block), place(2 * pair + 1, block))
        field[:, here] = value
        value = value.astype(f32)
        act[:, here] = (value * jax.nn.sigmoid(value)).astype(bf16)

    for at, out in ((core[0], keep), (1 - core[0], send)):
        lanes = pl.ds(pl.multiple_of(at * half, 128), half)
        out[:, :half] = act[:, lanes]
        out[:, half:] = cot[:, lanes]


def place_kernel(core, keep, came, block):
    depth, half = keep.shape[0], block.shape[2]
    for at, part in ((core[0], keep), (1 - core[0], came)):
        block[0, pl.ds(pl.multiple_of(at * depth, 16), depth), :] = part[:, :half]


def write_shifts(stack, values, taps=range(9)):
    depth = values.shape[0]
    for at, tap in enumerate(taps):
        row, col = offsets[tap]
        stack[pl.ds(at * depth, depth), :] = shifted(values, -row, -col)


def back_kernel(start, order, own, other, kernel_own, kernel_other, *refs):
    *sends, keep, stack_own, stack_other, block, held, sem = refs
    copy = pltpu.make_async_copy(kernel_own, held, sem)
    copy.start()
    half, depth, pixels = keep.shape
    places = [send.at[at] for send in sends for at in range(send.shape[0])]
    write_shifts(stack_own, own[:, start : start + pixels])
    write_shifts(stack_other, other[:, start : start + pixels])
    copy.wait()

    def step(at, _):
        lanes = pl.ds(pl.multiple_of(at * TILE, TILE), TILE)
        total = None
        for kernel, stack in ((held, stack_own), (kernel_other, stack_other)):
            part = lax.dot_general(
                kernel[...], stack[:, lanes], (((0,), (0,)), ((), ())), preferred_element_type=f32
            )
            total = part if total is None else total + part
        block[...] = total
        for slot in range(2 * half):
            rows = block[pl.ds(pl.multiple_of(order[slot] * depth, 8), depth), :]
            if slot < half:
                keep[slot, :, lanes] = rows
            else:
                places[slot - half][:, lanes] = rows.astype(bf16)
        return 0

    lax.fori_loop(0, pixels // TILE, step, 0)


def fetch(order, pieces, whole, sem):
    copies = []
    for piece in pieces:
        for at in range(piece.shape[0]):
            slot, depth = len(copies), piece.shape[1]
            start = pl.multiple_of(order[slot] * depth, 16)
            copies.append(
                pltpu.make_async_copy(piece.at[at], whole.at[pl.ds(start, depth), :], sem.at[slot])
            )
            copies[-1].start()
    return copies


def conv_tile(kernel, tile):
    depth = kernel.shape[0] // 9
    spread = jnp.dot(kernel[...], tile, preferred_element_type=f32)
    total = spread[4 * depth : 5 * depth]
    for tap, (row, col) in enumerate(offsets):
        if tap != 4:
            total = total + shifted(spread[tap * depth : (tap + 1) * depth], row, col)
    return total


def conv_one_kernel(
    core, order, three, beyond, kernel_own, kernel_other, bias_own, bias_other, whole, pre_own, pre_other, act, sem
):
    for copy in fetch(order, (three, beyond), whole, sem):
        copy.wait()
    depth = pre_own.shape[0]

    def step(at, _):
        lanes = pl.ds(pl.multiple_of(at * CONV_TILE, CONV_TILE), CONV_TILE)
        tile = whole[:, lanes]
        for kernel, bias, pre, place in (
            (kernel_own, bias_own, pre_own, core[0]),
            (kernel_other, bias_other, pre_other, 1 - core[0]),
        ):
            value = conv_tile(kernel, tile) + bias[:, :1].astype(f32)
            pre[:, lanes] = value
            rows = pl.ds(pl.multiple_of(place * depth, 16), depth)
            act[0, rows, lanes] = (value * jax.nn.sigmoid(value)).astype(bf16)
        return 0

    lax.fori_loop(0, whole.shape[1] // CONV_TILE, step, 0)


def conv_two_kernel(whole, kernel_own, kernel_other, out_own, out_other):
    def step(at, _):
        lanes = pl.ds(pl.multiple_of(at * CONV_TILE, CONV_TILE), CONV_TILE)
        tile = whole[:, lanes]
        out_own[:, lanes] = conv_tile(kernel_own, tile)
        out_other[:, lanes] = conv_tile(kernel_other, tile)
        return 0

    lax.fori_loop(0, whole.shape[1] // CONV_TILE, step, 0)


def slope_kernel(core, kept, near, far, pre_own, pre_other, own, other):
    depth = own.shape[0]
    for pre, place, out in ((pre_own, core[0], own), (pre_other, 1 - core[0], other)):
        rows = pl.ds(pl.multiple_of(place * depth, 16), depth)
        upstream = kept[0, rows, :] + near[0, rows, :].astype(f32) + far[0, rows, :].astype(f32)
        out[...] = (upstream * silu_slope(pre[...])).astype(bf16)


def write_grad(taps, parts, outs, grad, stacks):
    transposed = (((1,), (1,)), ((), ()))
    depth = parts[0][0].shape[0]
    rows = len(taps) * depth
    total = sums = None
    for at, (values, whole) in enumerate(parts):
        write_shifts(stacks.at[at], values, taps)
        part = lax.dot_general(stacks[at], whole[...], transposed, preferred_element_type=f32)
        total = part if total is None else total + part
        if taps[-1] == 8:
            ones = jnp.ones((EXTRA, values.shape[1]), bf16)
            part = lax.dot_general(ones, values, transposed, preferred_element_type=f32)
            sums = part if sums is None else sums + part
    grad[:rows, :] = total
    if taps[-1] == 8:
        grad[rows:, :] = jnp.zeros((EXTRA, grad.shape[1]), f32)
        grad[rows:, :depth] = sums
    base = 0
    for out in outs:
        size = out.shape[0]
        out[...] = grad[base : base + size, :].astype(bf16)
        base += size


def grad_one_kernel(taps, own, came, whole, whole_came, out, grad, stacks):
    parts = (own[...], whole), (came[...], whole_came)
    write_grad(taps, parts, (out,), grad, stacks)


def grad_two_kernel(core, cotangent, whole, whole_came, *refs):
    *outs, grad, stacks = refs
    half = whole.shape[1]
    own, came = (
        cotangent[:, pl.ds(pl.multiple_of(at * half, 128), half)] for at in (core[0], 1 - core[0])
    )
    parts = (own, whole), (came, whole_came)
    write_grad(tuple(range(9)), parts, outs, grad, stacks)


def copy_kernel(*refs):
    for values, out in zip(refs[: len(refs) // 2], refs[len(refs) // 2 :]):
        out[...] = values[...]


def add_kernel(left, right, out):
    out[...] = (left[...].astype(f32) + right[...].astype(f32)).astype(bf16)


def join_kernel(own, near, across, *refs):
    others, (joined, *outs) = refs[: len(refs) // 2 - 1], refs[len(refs) // 2 - 1 :]
    for at, block in enumerate((own, near, across)):
        joined[at] = block[0]
    for values, out in zip((near, *others), outs):
        out[...] = values[...]


def assemble_kernel(order, *refs):
    *pieces, whole, sem = refs
    for copy in fetch(order, pieces, whole, sem):
        copy.wait()


def sum_kernel(core, kept, near, far, own, other):
    depth = own.shape[0]
    for place, out in ((core[0], own), (1 - core[0], other)):
        rows = pl.ds(pl.multiple_of(place * depth, 16), depth)
        out[...] = kept[0, rows, :] + near[0, rows, :].astype(f32) + far[0, rows, :].astype(f32)


def output_kernel(core, field, own, came, bias, out, total, sem):
    half = own.shape[1]
    column = bias[:, :1].astype(f32)
    for at, part in ((core[0], own), (1 - core[0], came)):
        lanes = pl.ds(pl.multiple_of(at * half, 128), half)
        total[:, lanes] = (field[:, lanes].astype(f32) + part[...] + column).astype(bf16)
    copy = pltpu.make_async_copy(total, out, sem)
    copy.start()
    copy.wait()


def field_grad_kernel(core, field, cotangent, own, came, out, total, sem):
    half = own.shape[1]
    for at, part in ((core[0], own), (1 - core[0], came)):
        lanes = pl.ds(pl.multiple_of(at * half, 128), half)
        slope = silu_slope(field[:, lanes].astype(f32))
        total[:, lanes] = cotangent[:, lanes].astype(f32) + part[...] * slope
    copy = pltpu.make_async_copy(total, out, sem)
    copy.start()
    copy.wait()


def onward_kernel(keep, near, out):
    out[0] = (keep[1] + near[near.shape[0] - 1].astype(f32)).astype(bf16)


def finish_kernel(inner, *refs):
    pieces, (grad, bias, total, sem) = refs[:-4], refs[-4:]
    base, copies, rows = 0, [], grad.shape[0]
    for at, (made, came) in enumerate(zip(pieces[0::2], pieces[1::2])):
        size = made.shape[0]
        value = jnp.where(inner[0] == 1, made[...], came[...])
        total[base : base + size, :] = value.astype(f32)
        span = pl.ds(base, min(size, rows - base))
        copies.append(pltpu.make_async_copy(total.at[span, :], grad.at[span, :], sem.at[at]))
        copies[-1].start()
        base += size
    bias[...] = total[rows, : bias.shape[0]]
    for copy in copies:
        copy.wait()


def finish_first_kernel(inner, made, came, grad, total, sem):
    total[...] = jnp.where(inner[0] == 1, made[...], came[...]).astype(f32)
    copy = pltpu.make_async_copy(total, grad.at[pl.ds(0, total.shape[0]), :], sem)
    copy.start()
    copy.wait()


def finish_last_kernel(inner, made, came, begun, grad, bias, total, sem):
    total[...] = jnp.where(inner[0] == 1, made[...], came[...]).astype(f32)
    count = total.shape[0] - EXTRA
    rows = pl.ds(grad.shape[0] - count, count)
    copy = pltpu.make_async_copy(total.at[pl.ds(0, count), :], grad.at[rows, :], sem)
    copy.start()
    bias[...] = total[count, : bias.shape[0]]
    copy.wait()


SMEM = pl.BlockSpec(memory_space=pltpu.SMEM)
VMEM = pl.BlockSpec(memory_space=pltpu.VMEM)
ANY = pl.BlockSpec(memory_space=pl.ANY)
HBM = pl.BlockSpec(memory_space=pltpu.HBM)
SPACES = {id(VMEM): pltpu.VMEM, id(HBM): pltpu.HBM}


def in_hbm(values):
    return pltpu.with_memory_space_constraint(values, pltpu.HBM)


def run(body, name, ins, outs, scratch=(), out_specs=None, after=(), cost=0, aliases=None):
    count, total = len(ins), len(ins) + len(after)
    end = total + len(outs)

    def marked(*refs):
        body(*refs[:count], *refs[total:end], *refs[end + 1 :])
        refs[end][...] = jnp.zeros_like(refs[end])

    ins = list(ins) + [(VMEM, value) for value in after]
    args = [
        pltpu.with_memory_space_constraint(arg, SPACES[id(spec)]) if id(spec) in SPACES else arg
        for spec, arg in ins
    ]
    out_specs = list(out_specs or [VMEM] * len(outs)) + [VMEM]
    outs = list(outs) + [jax.ShapeDtypeStruct((8, 128), f32)]
    return pl.pallas_call(
        marked,
        name=name,
        out_shape=[
            SPACES[id(spec)](out.shape, out.dtype) if id(spec) in SPACES else out
            for spec, out in zip(out_specs, outs)
        ],
        in_specs=[spec for spec, _ in ins],
        out_specs=out_specs,
        scratch_shapes=list(scratch),
        input_output_aliases=aliases or {},
        cost_estimate=pl.CostEstimate(flops=cost, bytes_accessed=0, transcendentals=0),
        compiler_params=pltpu.CompilerParams(vmem_limit_bytes=VMEM_LIMIT),
    )(*args)


def split_local(
    groups, width, noise, buffer, reinit, slots, kernel_one, bias_one, kernel_two, bias_two, cotangent
):
    depth, pixels = noise.shape
    channels = kernel_one.shape[2]
    half = pixels // 2
    chips = width // 2
    block = 2 * depth
    rows = 9 * depth
    index = lax.axis_index("blk")
    core = index % 2
    chip = index // 2
    group = lax.axis_index("dp")
    shape = jax.ShapeDtypeStruct
    dma = pltpu.SemaphoreType.DMA

    first = [2, 4]

    def swap(values, axis, pairs, name):
        with jax.named_scope(name):
            return lax.ppermute(values, axis, pairs)

    def chip_swap(values, step, name):
        pairs = [(i, i ^ first[(step + i) % 2]) for i in range(width)]
        return swap(values, "blk", pairs, name)

    def core_swap(values, name):
        return swap(values, "blk", [(i, i ^ 1) for i in range(width)], name)

    line = {"in": [(0, 1), (3, 2)], "middle": [(1, 2), (2, 1)], "out": [(1, 0), (2, 3)]}

    def group_send(values, way, name):
        return swap(values, "dp", line[way], name + "_" + way)

    def order_of(which):
        swapped = jnp.where(which == 0, jnp.array([0, 1, 2, 3]), jnp.array([0, 2, 1, 3]))
        return jnp.bitwise_xor(chip, swapped).astype(jnp.int32)

    order, order_came = order_of(core), order_of(1 - core)
    core_at = core.reshape(1).astype(jnp.int32)
    inner = ((group == 1) | (group == 2)).reshape(1).astype(jnp.int32)

    def vmem(*values):
        return [(VMEM, value) for value in values]

    def like(*values):
        return [shape(value.shape, bf16) for value in values]

    own_one = kernel_one.reshape(rows, channels)
    own_two = kernel_two.reshape(rows, channels)
    other_two = core_swap(own_two, "kernel_two")
    other_one = core_swap(own_one, "kernel_one")
    bias_own = jnp.broadcast_to(bias_one[:, None], (depth, 128))
    bias_other = core_swap(bias_own, "bias")

    marks, phase = [], ["early"]

    def step(body, name, ins, outs, scratch=(), out_specs=None, also=(), aliases=None):
        after = marks[-1:] + list(also)
        costs = COSTS[phase[0]]
        cost = costs.get(name, costs["small" if name.split("_")[0] in SMALL else "big"])
        *results, mark = run(body, name, ins, outs, scratch, out_specs, after, cost, aliases)
        marks.append(mark)
        return results[0] if len(results) == 1 else results

    part = shape((depth, half), bf16)
    piece = shape((1, block, half), bf16)
    wide = shape((depth, pixels), bf16)
    field, keep, send = step(
        field_kernel,
        "field",
        [(SMEM, core_at)] + [(HBM, v) for v in (reinit, slots, noise, buffer, cotangent)],
        [wide, wide, wide],
        [
            pltpu.VMEM(noise.shape, bf16),
            pltpu.VMEM(buffer.shape, bf16),
            pltpu.VMEM(cotangent.shape, bf16),
            pltpu.VMEM(noise.shape, bf16),
            pltpu.SMEM(reinit.shape, jnp.int32),
            pltpu.SMEM(slots.shape, jnp.int32),
            dma((5,)),
        ],
    )
    came = core_swap(send, "pair")
    zero = step(place_kernel, "place", [(SMEM, core_at)] + vmem(keep, came), [piece])
    zero_near, zero_across = chip_swap(zero, 0, "zero_near"), chip_swap(zero, 1, "zero_across")

    def back(name, start, sends, *values):
        return step(
            functools.partial(back_kernel, start),
            name,
            [(SMEM, order)]
            + vmem(*values[:2])
            + [(HBM, in_hbm(values[2])), (VMEM, values[3])],
            [shape((count, block, half), bf16) for count in sends]
            + [shape((chips // 2, block, half), f32)],
            [
                pltpu.VMEM((rows, half), bf16),
                pltpu.VMEM((rows, half), bf16),
                pltpu.VMEM((channels, TILE), f32),
                pltpu.VMEM((rows, channels), bf16),
                dma,
            ],
        )

    send, last, keep_two = back("back_two", half, (1, 1), keep, came, own_two, other_two)
    last_two = chip_swap(last, 1, "two_last")
    zero, zero_near, send = step(
        join_kernel,
        "join_1",
        vmem(zero, zero_near, zero_across, send),
        [shape((3, block, half), bf16)] + like(zero_near, send),
        also=[other_one, bias_other],
    )
    zero_beyond = chip_swap(zero_near, 1, "zero_beyond")
    zero_came = core_swap(zero, "zero_pair")
    onward = step(onward_kernel, "onward_1", vmem(keep_two, last_two), [piece])
    far_two = chip_swap(onward, 0, "two_far")
    send, field = step(copy_kernel, "copy_1", vmem(send, field), like(send, field))
    near_two = chip_swap(send, 1, "two_near")
    zero_beyond = step(copy_kernel, "copy_2", vmem(zero_beyond), like(zero_beyond))
    beyond_came = core_swap(zero_beyond, "zero_pair_beyond")

    whole = shape((channels, half), bf16)
    plane = shape((depth, half), f32)
    whole_zero, pre_own, pre_other, one = step(
        conv_one_kernel,
        "conv_one",
        [(SMEM, core_at), (SMEM, order)]
        + vmem(zero, zero_beyond)
        + vmem(own_one, other_one, bias_own, bias_other),
        [whole, plane, plane, piece],
        [dma((chips,))],
    )

    pre_grad, pre_grad_send = step(
        slope_kernel,
        "slope",
        [(SMEM, core_at)] + vmem(keep_two, near_two, far_two, pre_own, pre_other),
        [part, part],
    )
    pre_grad_came = core_swap(pre_grad_send, "pre_grad")
    whole_zero_came = step(
        assemble_kernel,
        "assemble_1",
        [(SMEM, order_came)] + vmem(zero_came, beyond_came),
        [whole],
        [dma((chips,))],
    )

    def sizes(taps):
        return len(taps) * depth + (EXTRA if taps[-1] == 8 else 0)

    def grad_outs(taps):
        return [shape((sizes(taps), channels), bf16)]

    def grad_scratch(taps):
        return [
            pltpu.VMEM((sizes(taps), channels), f32),
            pltpu.VMEM((2, len(taps) * depth, half), bf16),
        ]

    def parts(ends):
        return [tuple(range(start, end)) for start, end in zip((0,) + ends[:-1], ends)]

    def add(name, left, right):
        return step(add_kernel, "add_" + name, vmem(left, right), like(left))

    phase[0] = "late"
    grads = []
    for at, taps in enumerate(parts(PARTS_ONE)):
        send = step(
            functools.partial(grad_one_kernel, taps),
            "grad_one_" + "ab"[at],
            vmem(pre_grad, pre_grad_came, whole_zero, whole_zero_came),
            grad_outs(taps),
            grad_scratch(taps),
        )
        grads.append(send)
        if at == 0:
            one = step(copy_kernel, "copy_3", vmem(one), like(one))
            one_near, one_across = chip_swap(one, 0, "one_near"), chip_swap(one, 1, "one_across")
    near_a = group_send(grads[0], "in", "one_a")
    send, keep_one = back("back_one", 0, (2,), pre_grad, pre_grad_send, own_one, other_one)
    send_one = send
    three, one_near = step(
        join_kernel,
        "join_one",
        vmem(one, one_near, one_across),
        [shape((3, block, half), bf16)] + like(one_near),
    )
    one_beyond = chip_swap(one_near, 1, "one_beyond")
    three_came = core_swap(three, "one_pair")

    send_b = step(copy_kernel, "copy_4", vmem(grads[1]), like(grads[1]))
    near_b = group_send(send_b, "in", "one_b")
    mine_a = add("one_a", grads[0], near_a)
    far_a = group_send(mine_a, "middle", "one_a")

    one_beyond = step(copy_kernel, "copy_beyond_one", vmem(one_beyond), like(one_beyond))
    beyond_came = core_swap(one_beyond, "one_pair_beyond")
    whole_one = step(
        assemble_kernel,
        "assemble_one",
        [(SMEM, order)] + vmem(three, one_beyond),
        [whole],
        [dma((chips,))],
    )
    whole_one_came = step(
        assemble_kernel,
        "assemble_one_came",
        [(SMEM, order_came)] + vmem(three_came, beyond_came),
        [whole],
        [dma((chips,))],
    )

    send_a, keep_b = step(
        grad_two_kernel,
        "grad_two",
        [(SMEM, core_at)] + vmem(cotangent, whole_one, whole_one_came),
        [out for taps in parts(PARTS_TWO) for out in grad_outs(taps)],
        grad_scratch(tuple(range(9))),
    )
    near_a = group_send(send_a, "in", "two_a")
    mine_b = add("one_b", send_b, near_b)
    far_b = group_send(mine_b, "middle", "one_b")
    send_b = step(copy_kernel, "copy_6", vmem(keep_b), like(keep_b))
    near_b = group_send(send_b, "in", "two_b")
    half_a = add("one_a_half", mine_a, far_a)
    rest_a = group_send(half_a, "out", "one_a")
    out_own, out_other = step(
        conv_two_kernel, "conv_two", vmem(whole_one, own_two, other_two), [plane, plane]
    )
    mine_two_a = add("two_a", send_a, near_a)
    far_two_a = group_send(mine_two_a, "middle", "two_a")
    half_b = add("one_b_half", mine_b, far_b)
    rest_b = group_send(half_b, "out", "one_b")
    mine_two_b = add("two_b", send_b, near_b)
    far_two_b = group_send(mine_two_b, "middle", "two_b")
    rest_a = step(copy_kernel, "copy_7", vmem(rest_a), like(rest_a))
    send_one = step(copy_kernel, "copy_5", vmem(send_one), like(send_one))
    near_one = chip_swap(send_one, 1, "one_near")
    half_two_a = add("two_a_half", mine_two_a, far_two_a)
    rest_two_a = group_send(half_two_a, "out", "two_a")

    def finish(name, pieces):
        kernel_grad, bias_grad = step(
            finish_kernel,
            name,
            [(SMEM, inner)] + vmem(*pieces),
            [shape((rows, channels), f32), shape((depth,), f32)],
            [pltpu.VMEM((rows + EXTRA, channels), f32), dma((len(pieces) // 2,))],
            out_specs=[ANY, VMEM],
        )
        return kernel_grad.reshape(9, depth, channels), bias_grad

    kernel_grad_one, bias_grad_one = finish("finish_one", [half_a, rest_a, half_b, rest_b])
    half_two_b = add("two_b_half", mine_two_b, far_two_b)
    rest_two_b = group_send(half_two_b, "out", "two_b")
    onward = step(onward_kernel, "onward_2", vmem(keep_one, near_one), [piece])
    far_one = chip_swap(onward, 0, "one_far")
    out_other = step(copy_kernel, "copy_9", vmem(out_other), [plane])
    out_came = core_swap(out_other, "out_pair")
    own, other = step(
        sum_kernel, "sum", [(SMEM, core_at)] + vmem(keep_one, near_one, far_one), [plane, plane]
    )
    other = core_swap(other, "field_pair")
    begun = step(
        finish_first_kernel,
        "finish_two_first",
        [(SMEM, inner)] + vmem(half_two_a, rest_two_a),
        [shape((rows, channels), f32)],
        [pltpu.VMEM(half_two_a.shape, f32), dma],
        out_specs=[ANY],
    )
    output = step(
        output_kernel,
        "output",
        [(SMEM, core_at)]
        + vmem(field, out_own, out_came, jnp.broadcast_to(bias_two[:, None], (depth, 128))),
        [wide],
        [pltpu.VMEM((depth, pixels), bf16), dma],
        out_specs=[ANY],
    )
    grad_field = step(
        field_grad_kernel,
        "field_grad",
        [(SMEM, core_at)] + vmem(field, cotangent, own, other),
        [shape((depth, pixels), f32)],
        [pltpu.VMEM((depth, pixels), f32), dma],
        out_specs=[ANY],
    )
    count = half_two_b.shape[0]
    kernel_grad_two, bias_grad_two = step(
        finish_last_kernel,
        "finish_two",
        [(SMEM, inner)] + vmem(half_two_b, rest_two_b) + [(ANY, begun)],
        [shape((rows, channels), f32), shape((depth,), f32)],
        [pltpu.VMEM((count, channels), f32), dma],
        out_specs=[ANY, VMEM],
        aliases={3: 0},
    )
    kernel_grad_two = kernel_grad_two.reshape(9, depth, channels)
    return output, grad_field, kernel_grad_one, bias_grad_one, kernel_grad_two, bias_grad_two


def shift_tap(field, row, col):
    depth = field.shape[0]
    grid = field.reshape(depth, -1, 8, 8)
    grid = jnp.pad(grid, ((0, 0), (0, 0), (1, 1), (1, 1)))
    grid = grid[:, :, 1 + row : 9 + row, 1 + col : 9 + col]
    return grid.reshape(depth, -1)


def add_conv(total, piece, kernel):
    for number, (row, col) in enumerate(offsets):
        total = total + jnp.dot(
            kernel[number], shift_tap(piece, row, col), preferred_element_type=f32
        )
    return total


def add_grad(piece, upstream):
    parts = [
        lax.dot_general(
            upstream,
            shift_tap(piece, row, col),
            (((1,), (1,)), ((), ())),
            preferred_element_type=f32,
        )
        for row, col in offsets
    ]
    return jnp.stack(parts, 0)


def back_shifts(upstream):
    return jnp.stack([shift_tap(upstream, -row, -col) for row, col in offsets], 0)


def spread_rows(kernel, moved):
    return lax.dot_general(kernel, moved, (((0, 1), (0, 1)), ((), ())), preferred_element_type=f32)


def plain_local(
    noise, buffer, reinit, slots, kernel_one, bias_one, kernel_two, bias_two, cotangent
):
    depth = noise.shape[0]
    images = reinit.shape[0]
    pixels = images * 64
    stored = buffer.reshape(depth, -1, 64)[:, slots, :]
    fresh = noise.reshape(depth, images, 64)
    field = (
        jnp.where(reinit[None, :, None] == 1, fresh, stored).reshape(depth, pixels).astype(f32)
    )
    act_zero = jax.nn.silu(field).astype(bf16)
    empty = jnp.zeros((depth, pixels), f32)
    whole_zero = lax.all_gather(act_zero, "blk", axis=0, tiled=True)
    pre_one = add_conv(empty, whole_zero, kernel_one)
    pre_one = pre_one + bias_one.astype(f32)[:, None]
    act_one = jax.nn.silu(pre_one).astype(bf16)
    whole_one = lax.all_gather(act_one, "blk", axis=0, tiled=True)
    pre_two = add_conv(empty, whole_one, kernel_two)
    output = (field + pre_two + bias_two.astype(f32)[:, None]).astype(bf16)
    bias_grad_two = jnp.sum(cotangent.astype(f32), axis=1)
    kernel_grad_two = add_grad(whole_one, cotangent)
    grad_act_one = lax.psum_scatter(
        spread_rows(kernel_two, back_shifts(cotangent)), "blk", scatter_dimension=0, tiled=True
    )
    grad_pre_one = (grad_act_one * silu_slope(pre_one)).astype(bf16)
    bias_grad_one = jnp.sum(grad_pre_one.astype(f32), axis=1)
    kernel_grad_one = add_grad(whole_zero, grad_pre_one)
    grad_act_zero = lax.psum_scatter(
        spread_rows(kernel_one, back_shifts(grad_pre_one)).astype(bf16),
        "blk",
        scatter_dimension=0,
        tiled=True,
    ).astype(f32)
    grad_field = cotangent.astype(f32) + grad_act_zero * silu_slope(field)
    summed = lax.psum((kernel_grad_one, bias_grad_one, kernel_grad_two, bias_grad_two), "dp")
    return (output, grad_field, summed[0], summed[1], summed[2], summed[3])


def solution(mesh):
    groups, width = mesh.shape["dp"], mesh.shape["blk"]

    def local(noise, *rest):
        if groups == 4 and width == 8 and noise.shape[0] % 16 == 0 and noise.shape[1] % 512 == 0:
            return split_local(groups, width, noise, *rest)
        return plain_local(noise, *rest)

    return jax.shard_map(
        local,
        mesh=mesh,
        in_specs=(
            P("blk", "dp"),
            P("blk", "dp"),
            P("dp"),
            P("dp"),
            P(None, "blk", None),
            P("blk"),
            P(None, "blk", None),
            P("blk"),
            P("blk", "dp"),
        ),
        out_specs=(
            P("blk", "dp"),
            P("blk", "dp"),
            P(None, "blk", None),
            P("blk"),
            P(None, "blk", None),
            P("blk"),
        ),
        check_vma=False,
    )
```
